256 devices in a mesh: blk: 128 (over z, x, y_hi, core), span: 2 (over y_lo).
Axes of the slice: x: 4, y: 4 (y_hi: 2, y_lo: 2; y = y_hi * 2 + y_lo), z: 8, core: 2. Of those that a mesh axis runs over, the one named last changes fastest.
Arguments:
- theta_init: float32 [128, 16, 128, 256], P('blk', None, None, 'span'), may hold values from -5 to 5
- conductivity: float32 [128, 16, 128, 256], P('blk', None, None, 'span'), may hold values from 0.03 to 0.14
- velocity: float32 [128, 3, 16, 128, 256], P('blk', None, None, None, 'span'), may hold values from -0.05 to 0.05
- heat_source: float32 [128, 16, 128, 256], P('blk', None, None, 'span'), may hold values from -0.25 to 0.25
- wall_init: float32 [128, 128, 256], P('blk', None, 'span'), may hold values from -1.5 to 1.5
- block_type: int32 [128], replicated, may hold values from 0 to 1, as said below
- partner_block: int32 [128, 128], P('blk'), may hold values from 0 to 127, as said below
- partner_row: int32 [128, 128], P('blk'), may hold values from 0 to 127
Outputs:
- temperature: float32 [128, 16, 128, 256], P('blk', None, None, 'span')
- wall_row: float32 [128, 128, 256], P('blk', None, 'span')
The draws below stay inside these ranges and needn't reach their ends.
Inputs may be any that keep to these rules, and one draw needn't show every extreme that they name: `block_type`: exactly 64 blocks are fluid. `partner_block`: the partner block is always of the other type and the matching is mutual: the partner row's partner is the row itself; each block has exactly 2 wall rows that face each block of the other type.
All inputs are finite; a program needn't handle non-finite values.
Results may differ from the reference program's by a relative error of at most 0.0003.
Values sent between devices are 32-bit elements; how exact they have to be, the bound alone decides.
A program may use at most 128 MiB of HBM per device.

```python
import math
import jax
import jax.numpy as jnp
from jax import lax

CY = 16
CX = 128
SWEEPS = 3
ITERS = 2
BLOCKS = 128
CZ = 256


def layout(key):
    half = BLOCKS // 2
    capacity = CX // half
    order = jax.random.permutation(jax.random.fold_in(key, 11), BLOCKS).astype(jnp.int32)
    offsets = jax.random.randint(jax.random.fold_in(key, 12), (BLOCKS,), 0, CX).astype(jnp.int32)
    twist = jax.random.randint(jax.random.fold_in(key, 13), (), 0, half).astype(jnp.int32)
    inverse = jnp.zeros((BLOCKS,), jnp.int32).at[order].set(jnp.arange(BLOCKS, dtype=jnp.int32))
    fluid = inverse < half
    within = jnp.where(fluid, inverse, inverse - half)
    rows = jnp.arange(CX, dtype=jnp.int32)
    logical = (rows[None, :] - offsets[:, None]) % CX
    group = logical // capacity
    slot = logical % capacity
    metal_index = (within[:, None] + group + twist) % half
    block_f = order[half + metal_index]
    row_f = within[:, None] * capacity + slot
    fluid_group = (within[:, None] - group - twist) % half
    block_m = order[group]
    row_m = fluid_group * capacity + slot
    partner = jnp.where(fluid[:, None], block_f, block_m).astype(jnp.int32)
    drawn_row = jnp.where(fluid[:, None], row_f, row_m).astype(jnp.int32)
    partner_rows = ((drawn_row + offsets[partner]) % CX).astype(jnp.int32)
    return (fluid.astype(jnp.int32), partner, partner_rows)


def draw_block_type(key, part):
    shared = layout(key)
    return shared[0]


def draw_partner_block(key, part):
    shared = layout(key)
    return shared[1]


def draw_partner_row(key, part):
    shared = layout(key)
    return shared[2]


def steps_of(rng, dims, cuts, smallest, top_value):
    factor_of, own = 1.0, jax.random.fold_in(rng, 6)
    for axis_at, blocks in cuts:
        draws = jnp.exp(jax.random.uniform(jax.random.fold_in(own, axis_at), (blocks,), jnp.float32, smallest / len(cuts), top_value / len(cuts)))
        factor_of = factor_of * jnp.repeat(draws, dims[axis_at] // blocks).reshape([-1 if axis == axis_at else 1 for axis in range(len(dims))])
    return factor_of


def bell_draw(rng, shape, spread, reach, cuts=(), kind=jnp.bfloat16):
    array = jax.random.normal(rng, shape, jnp.float32) * spread
    if len(cuts) > 0:
        array = steps_of(rng, shape, cuts, -0.22, 0.18) * array
    return jnp.clip(array, min=-reach, max=reach).astype(kind)


def setup_inputs(seed: int = 0) -> dict:
    arg_keys = jax.random.split(jax.random.key(seed), 9)
    return {
        "theta_init": bell_draw(arg_keys[0], (BLOCKS, CY, CX, CZ), 1.0, 5.0, ((0, 128), (3, 2)), jnp.float32),
        "conductivity": jnp.clip(jnp.exp(math.log(0.14) - 1.5404451 * jax.random.uniform(arg_keys[1], (BLOCKS, CY, CX, CZ), jnp.float32) ** steps_of(arg_keys[1], (BLOCKS, CY, CX, CZ), ((0, 128), (3, 2)), -0.2, 0.2)), 0.03, 0.14),
        "velocity": jnp.clip(jax.random.uniform(arg_keys[2], (BLOCKS, 3, CY, CX, CZ), jnp.float32, -0.05, 0.05) * steps_of(arg_keys[2], (BLOCKS, 3, CY, CX, CZ), ((0, 128), (4, 2)), -0.4, 0.0), -0.05, 0.05),
        "heat_source": bell_draw(arg_keys[3], (BLOCKS, CY, CX, CZ), 0.05, 0.25, ((0, 128), (3, 2)), jnp.float32),
        "wall_init": bell_draw(arg_keys[4], (BLOCKS, CX, CZ), 0.3, 1.5, ((0, 128), (2, 2)), jnp.float32),
        "block_type": draw_block_type(jax.random.fold_in(arg_keys[8], 71), 0),
        "partner_block": draw_partner_block(jax.random.fold_in(arg_keys[8], 71), 0),
        "partner_row": draw_partner_row(jax.random.fold_in(arg_keys[8], 71), 0),
    }


def advance(field, cond, vel_mid, src_mid, wall_mid, fluid_cols):
    center = field[:, 1:-1, 1:-1]
    cond_mid = cond[:, 1:-1, 1:-1]
    fluid_mid = fluid_cols[1:-1]
    same_west = (fluid_cols[:-2] == fluid_mid).astype(jnp.float32)[None, :, None]
    same_east = (fluid_cols[2:] == fluid_mid).astype(jnp.float32)[None, :, None]
    west = same_west * field[:, :-2, 1:-1] + (1.0 - same_west) * center
    east = same_east * field[:, 2:, 1:-1] + (1.0 - same_east) * center
    south = field[:, 1:-1, :-2]
    north = field[:, 1:-1, 2:]
    k_west = 0.5 * (cond_mid + cond[:, :-2, 1:-1])
    k_east = 0.5 * (cond_mid + cond[:, 2:, 1:-1])
    k_south = 0.5 * (cond_mid + cond[:, 1:-1, :-2])
    k_north = 0.5 * (cond_mid + cond[:, 1:-1, 2:])
    fluid_row = fluid_mid[:, None]
    ghost = fluid_row * wall_mid + (1.0 - fluid_row) * center[0]
    below = jnp.concatenate([ghost[None], center[:-1]], 0)
    above = jnp.concatenate([center[1:], center[-1:]], 0)
    cond_pair = 0.5 * (cond_mid[1:] + cond_mid[:-1])
    k_below = jnp.concatenate([cond_mid[:1], cond_pair], 0)
    k_above = jnp.concatenate([cond_pair, cond_mid[-1:]], 0)
    diffusion = (k_west * (west - center) + k_east * (east - center) + k_south * (south - center)
                 + k_north * (north - center) + k_below * (below - center) + k_above * (above - center))
    flow = vel_mid * fluid_mid[None, None, :, None]
    along = flow[0]
    normal = flow[1]
    spanwise = flow[2]
    transport = (jnp.maximum(along, 0.0) * (center - west) + jnp.minimum(along, 0.0) * (east - center)
                 + jnp.maximum(normal, 0.0) * (center - below) + jnp.minimum(normal, 0.0) * (above - center)
                 + jnp.maximum(spanwise, 0.0) * (center - south) + jnp.minimum(spanwise, 0.0) * (north - center))
    inflow = (1.0 - fluid_row) * wall_mid
    heated = jnp.concatenate([inflow[None], jnp.zeros_like(center[1:])], 0)
    return center + diffusion - transport + src_mid + heated


def reference(theta_init, conductivity, velocity, heat_source, wall_init, block_type, partner_block, partner_row):
    kinds = block_type.astype(jnp.float32)

    def one_block(index, field, wall):
        before = (index - 1) % BLOCKS
        after = (index + 1) % BLOCKS

        def extended(whole):
            joined = jnp.concatenate([whole[before][..., -1:, :], whole[index], whole[after][..., :1, :]], axis=-2)
            return jnp.concatenate([joined[..., -1:], joined, joined[..., :1]], axis=-1)

        fluid_cols = jnp.concatenate([kinds[before][None], jnp.full((CX,), kinds[index]), kinds[after][None]])
        return advance(extended(field), extended(conductivity), velocity[index], heat_source[index], wall[index], fluid_cols)

    theta = theta_init
    wall = wall_init
    for repeat in range(ITERS):
        for sweep_index in range(SWEEPS):
            theta = lax.map(lambda index: one_block(index, theta, wall), jnp.arange(BLOCKS, dtype=jnp.int32))
        is_fluid = kinds[:, None, None] > 0.5
        sent = jnp.where(is_fluid, conductivity[:, 0] * (theta[:, 0] - wall), theta[:, 0])
        wall = sent[partner_block, partner_row]
    return theta, wall
```

```python
import functools

import jax
import jax.numpy as jnp
from jax import lax
from jax.experimental import pallas as pl
from jax.experimental.pallas import tpu as pltpu
from jax.sharding import PartitionSpec as P

MESH = pl.DeviceIdType.MESH
SWEEPS = 3
CY, CX, LZ = 16, 128, 128
TILES = CX // 8 + 1
ROWS = 8 * TILES
PAD = ROWS + 16
F32 = jnp.float32
AW, AE, AS, AN, AB, AA, AD, SRC = range(8)


def tile(i, shift=0):
    return pl.ds(8 + 8 * i + shift, 8)


def row8(i):
    return pl.ds(8 * i, 8)


def remote(src, dst, send, recv, device):
    return pltpu.make_async_remote_copy(
        src_ref=src, dst_ref=dst, send_sem=send, recv_sem=recv, device_id=device, device_id_type=MESH
    )


def split3(x):
    hi = x.astype(jnp.bfloat16)
    rest = x - hi.astype(F32)
    mid = rest.astype(jnp.bfloat16)
    low = (rest - mid.astype(F32)).astype(jnp.bfloat16)
    return hi, mid, low


def pick(chooser, x):
    return sum(jnp.dot(chooser, part, preferred_element_type=F32) for part in split3(x))


def kernel(
    n, theta_ref, cond_ref, vel_ref, heat_ref, wall_ref, kind_ref, block_ref, row_ref,
    theta_out, wall_out,
    th, kb, vb, hb, co, st, sk, sv, sco, sw, pz,
    xs, xr, qs, qr, cr, wx, wp, wc, tr, q1, q1r, c1r,
    sb, rb, choose_send, choose_recv,
    load_sem, send_sem, recv_sem, many_send, many_recv,
):
    b, s = lax.axis_index("blk"), lax.axis_index("span")
    chunk = 2 * CX // n
    east, west = lax.rem(b + 1, n), lax.rem(b + n - 1, n)
    E, W, Z, ZE, ZW = (east, s), (west, s), (b, 1 - s), (east, 1 - s), (west, 1 - s)

    loads = [
        pltpu.make_async_copy(theta_ref.at[0], th.at[0, pl.ds(1, CY), pl.ds(8, CX)], load_sem.at[0]),
        pltpu.make_async_copy(cond_ref.at[0], kb.at[:, pl.ds(8, CX)], load_sem.at[1]),
        pltpu.make_async_copy(vel_ref.at[0], vb.at[:, :, pl.ds(0, CX)], load_sem.at[2]),
        pltpu.make_async_copy(heat_ref.at[0], hb.at[:, pl.ds(0, CX)], load_sem.at[3]),
        pltpu.make_async_copy(wall_ref.at[0], th.at[0, 0, pl.ds(8, CX)], load_sem.at[4]),
    ]
    for load in loads:
        load.start()

    rb[:, pl.ds(b, 1)] = jnp.zeros((2, 1, chunk, LZ), F32)

    barrier = pltpu.get_barrier_semaphore()

    def greet(d, carry):
        pl.semaphore_signal(barrier, inc=1, device_id=(lax.rem(b + d, n), s), device_id_type=MESH)
        return carry

    lax.fori_loop(1, n, greet, 0)
    for peer in (Z, ZE, ZW):
        pl.semaphore_signal(barrier, inc=1, device_id=peer, device_id_type=MESH)

    fluid = kind_ref[b].astype(F32)
    metal = 1.0 - fluid
    same_west = 1.0 - jnp.abs(kind_ref[west].astype(F32) - fluid)
    same_east = 1.0 - jnp.abs(kind_ref[east].astype(F32) - fluid)

    lane = lax.broadcasted_iota(jnp.int32, (8, LZ), 1)
    sub = lax.broadcasted_iota(jnp.int32, (8, LZ), 0)
    group, place = lane // 8, lane % 8
    first_lane, last_lane = lane == 0, lane == LZ - 1
    low_half = place < 4
    middle = (place >= 2) & (place < 6)

    mine = jnp.broadcast_to(block_ref[...].astype(F32), (CX, CX))
    theirs = jnp.broadcast_to(row_ref[...].astype(F32), (CX, CX))
    mine_t, theirs_t = mine.T, theirs.T
    at_row = lax.broadcasted_iota(jnp.int32, (CX, CX), 0)
    at_col = lax.broadcasted_iota(jnp.int32, (CX, CX), 1)
    alike = mine_t == mine
    rank = jnp.sum(jnp.where(alike & (at_row < at_col), 1.0, 0.0), axis=0, keepdims=True)
    code = (chunk * mine[0:1] + rank).astype(jnp.int32)
    choose_send[...] = jnp.where(
        lax.broadcasted_iota(jnp.int32, (2 * CX, CX), 0) == code, 1.0, 0.0
    ).astype(jnp.bfloat16)
    rank_t = jnp.sum(jnp.where(alike & (theirs < theirs_t), 1.0, 0.0), axis=1, keepdims=True)
    code_t = (chunk * mine_t[:, 0:1] + rank_t).astype(jnp.int32)
    choose_recv[...] = jnp.where(
        lax.broadcasted_iota(jnp.int32, (CX, 2 * CX), 1) == code_t, 1.0, 0.0
    ).astype(jnp.bfloat16)

    for p in range(2):
        th[p, CY + 1] = jnp.zeros((PAD, LZ), F32)

    for load in loads:
        load.wait()

    def edges(load):
        out = pltpu.roll(load(0), 4, 1)
        for y in range(1, CY):
            out = jnp.where(group == y, pltpu.roll(load(y), (8 * y + 4) % LZ, 1), out)
        return out

    def pack_six(i, at, at_pad):
        q_th = edges(lambda y: th[0, y + 1, at_pad])
        q_k = edges(lambda y: kb[y, at_pad])
        q_v = [edges(lambda y, d=d: vb[d, y, at]) for d in range(3)]
        q_h = edges(lambda y: hb[y, at])
        return (
            q_th,
            q_k,
            jnp.where(middle, q_v[0], pltpu.roll(q_v[1], 4, 1)),
            jnp.where(middle, q_v[2], pltpu.roll(q_h, 4, 1)),
        )

    def pack_tile(i, carry):
        at = pl.ds(pl.multiple_of(8 * i, 8), 8)
        at_pad = pl.ds(pl.multiple_of(8 * i + 8, 8), 8)
        for slot, q in enumerate(pack_six(i, at, at_pad)):
            qs[slot, at] = q
        return carry

    lax.fori_loop(0, TILES - 1, pack_tile, 0)

    def pack_rows(y, carry):
        last, pad_last = pl.ds(CX - 8, 8), pl.ds(CX, 8)
        xs[0, 0, y] = jnp.where(sub >= 5, th[0, y + 1, pad_last], pltpu.roll(kb[y, pad_last], 5, 0))
        xs[0, 1, y] = jnp.where(
            sub >= 6,
            vb[0, y, last],
            jnp.where(
                sub >= 4,
                pltpu.roll(vb[1, y, last], 6, 0),
                jnp.where(sub >= 2, pltpu.roll(vb[2, y, last], 4, 0), pltpu.roll(hb[y, last], 2, 0)),
            ),
        )
        zero, pad_zero = pl.ds(0, 8), pl.ds(8, 8)
        xs[1, 0, y] = jnp.where(sub < 3, th[0, y + 1, pad_zero], pltpu.roll(kb[y, pad_zero], 3, 0))
        xs[1, 1, y] = jnp.where(
            sub < 2,
            vb[0, y, zero],
            jnp.where(
                sub < 4,
                pltpu.roll(vb[1, y, zero], 2, 0),
                jnp.where(sub < 6, pltpu.roll(vb[2, y, zero], 4, 0), pltpu.roll(hb[y, zero], 6, 0)),
            ),
        )
        return carry

    lax.fori_loop(0, CY, pack_rows, 0)

    pl.semaphore_wait(barrier, n + 2)

    def wall_copies(r, plane, base):
        tail, head = plane.at[pl.ds(CX, 8)], plane.at[pl.ds(8, 8)]
        return [
            remote(tail, wx.at[r, 0], send_sem.at[base], recv_sem.at[base], E),
            remote(head, wx.at[r, 1], send_sem.at[base + 1], recv_sem.at[base + 1], W),
            remote(plane.at[pl.ds(8, CX)], wp.at[r], send_sem.at[base + 2], recv_sem.at[base + 2], Z),
            remote(tail, wc.at[r, 0], send_sem.at[base + 3], recv_sem.at[base + 3], ZE),
            remote(head, wc.at[r, 1], send_sem.at[base + 4], recv_sem.at[base + 4], ZW),
        ]

    copies = [
        remote(xs.at[0], xr.at[0], send_sem.at[0], recv_sem.at[0], E),
        remote(xs.at[1], xr.at[1], send_sem.at[1], recv_sem.at[1], W),
        remote(qs.at[:, pl.ds(CX - 8, 8)], cr.at[0], send_sem.at[3], recv_sem.at[3], ZE),
        remote(qs.at[:, pl.ds(0, 8)], cr.at[1], send_sem.at[4], recv_sem.at[4], ZW),
        remote(qs, qr, send_sem.at[2], recv_sem.at[2], Z),
    ] + wall_copies(0, th.at[0, 0], 5)
    for copy in copies:
        copy.start()
    for copy in copies:
        copy.wait()

    last = TILES - 1
    rows_last = row8(last)

    def unpack_rows(y, carry):
        e0, e1, w0, w1 = xr[1, 0, y], xr[1, 1, y], xr[0, 0, y], xr[0, 1, y]
        near = sub < 4
        t = jnp.where(near, e0, w0)
        th[0, y + 1, tile(last)] = t
        th[0, y + 1, tile(-1)] = t
        th[0, y + 1, tile(TILES)] = th[0, y + 1, tile(0)]
        k = jnp.where(near, pltpu.roll(e0, 5, 0), pltpu.roll(w0, 3, 0))
        kb[y, tile(last)] = k
        kb[y, tile(-1)] = k
        kb[y, tile(TILES)] = kb[y, tile(0)]
        vb[0, y, rows_last] = jnp.where(near, e1, w1)
        vb[1, y, rows_last] = jnp.where(near, pltpu.roll(e1, 6, 0), pltpu.roll(w1, 2, 0))
        vb[2, y, rows_last] = jnp.where(near, pltpu.roll(e1, 4, 0), pltpu.roll(w1, 4, 0))
        hb[y, rows_last] = jnp.where(near, pltpu.roll(e1, 2, 0), pltpu.roll(w1, 6, 0))
        return carry

    lax.fori_loop(0, CY, unpack_rows, 0)

    def put_strip(ref, i, own, other):
        for side in range(2):
            value = jnp.where(low_half, other, own) if side == 0 else jnp.where(low_half, own, other)
            ref[side, tile(i)] = value
            if i == last:
                ref[side, tile(-1)] = value
            if i == 0:
                ref[side, tile(TILES)] = value

    def strip_wall(r, p):
        th[p, 0, tile(last)] = jnp.where(sub < 4, wx[r, 1], wx[r, 0])
        th[1 - p, 0, pl.ds(8, ROWS)] = th[p, 0, pl.ds(8, ROWS)]
        for i in range(TILES):
            own = pltpu.roll(th[p, 0, tile(i)], 4, 1)
            other = wp[r, row8(i)] if i < last else jnp.where(sub < 4, wc[r, 1], wc[r, 0])
            other = pltpu.roll(other, 4, 1)
            sw[0, row8(i)] = jnp.where(low_half, other, own)
            sw[1, row8(i)] = jnp.where(low_half, own, other)

    halo_q = pack_six(last, rows_last, tile(last))
    for i in range(TILES):
        own = [qs[slot, row8(i)] for slot in range(4)] if i < last else halo_q
        other = [
            qr[slot, row8(i)] if i < last else jnp.where(sub < 4, cr[1, slot], cr[0, slot])
            for slot in range(4)
        ]
        put_strip(st.at[0], i, own[0], other[0])
        put_strip(sk, i, own[1], other[1])
        for slot in (2, 3):
            for part in range(2):
                o, t = own[slot], other[slot]
                if part:
                    o, t = pltpu.roll(o, LZ - 4, 1), pltpu.roll(t, LZ - 4, 1)
                at = 2 * (slot - 2) + part
                sv[at, 0, row8(i)] = jnp.where(low_half, t, o)
                sv[at, 1, row8(i)] = jnp.where(low_half, o, t)
    strip_wall(0, 0)

    def face_masks(i, a_w, a_e):
        if i == 0:
            a_w = jnp.where(sub == 0, same_west * a_w, a_w)
        if i == last - 1:
            a_e = jnp.where(sub == 7, same_east * a_e, a_e)
        return a_w, a_e

    def coefficients(k, k_w, k_e, k_s, k_n, k_b, k_a, v, i, bottom, top):
        v = [fluid * x for x in v]
        a_w = 0.5 * (k + k_w) + jnp.maximum(v[0], 0.0)
        a_e = 0.5 * (k + k_e) - jnp.minimum(v[0], 0.0)
        a_w, a_e = face_masks(i, a_w, a_e)
        a_b = 0.5 * (k + k_b) + jnp.maximum(v[1], 0.0)
        a_b = a_b * (1.0 - metal * bottom)
        a_a = (0.5 * (k + k_a) - jnp.minimum(v[1], 0.0)) * (1.0 - top)
        a_s = 0.5 * (k + k_s) + jnp.maximum(v[2], 0.0)
        a_n = 0.5 * (k + k_n) - jnp.minimum(v[2], 0.0)
        a_d = 1.0 - (a_w + a_e + a_s + a_n + a_b + a_a)
        return a_w, a_e, a_s, a_n, a_b + metal * bottom, a_a, a_d

    strip_bottom = (group == 0).astype(F32)
    strip_top = (group == CY - 1).astype(F32)
    for side in range(2):
        for i in range(TILES):
            k = sk[side, tile(i)]
            k_b = jnp.where(group == 0, k, pltpu.roll(k, 8, 1))
            a = coefficients(
                k, sk[side, tile(i, -1)], sk[side, tile(i, 1)], pltpu.roll(k, 1, 1), pltpu.roll(k, LZ - 1, 1),
                k_b, pltpu.roll(k, LZ - 8, 1), [sv[d, side, row8(i)] for d in range(3)], i, strip_bottom, strip_top,
            )
            for slot, value in enumerate(a):
                sco[slot, side, row8(i)] = value
            sco[SRC, side, row8(i)] = sv[3, side, row8(i)]

    def join(ref):
        for i in range(TILES):
            pz[row8(i)] = jnp.where(place == 3, ref[0, tile(i)], ref[1, tile(i)])

    join(sk)

    def span_neighbours(c, z, y):
        z = pltpu.roll(z, 124 - 8 * y, 1)
        return (
            pltpu.roll(jnp.where(last_lane, z, c), 1, 1),
            pltpu.roll(jnp.where(first_lane, z, c), LZ - 1, 1),
        )

    def plane_coefficients(y, carry):
        bottom = (y == 0).astype(F32)
        top = (y == CY - 1).astype(F32)
        below, above = jnp.maximum(y - 1, 0), jnp.minimum(y + 1, CY - 1)
        for i in range(TILES):
            k = kb[y, tile(i)]
            k_s, k_n = span_neighbours(k, pz[row8(i)], y)
            a = coefficients(
                k, kb[y, tile(i, -1)], kb[y, tile(i, 1)], k_s, k_n, kb[below, tile(i)], kb[above, tile(i)],
                [vb[d, y, row8(i)] for d in range(3)], i, bottom, top,
            )
            for slot, value in enumerate(a):
                co[slot, y, row8(i)] = value
        return carry

    lax.fori_loop(0, CY, plane_coefficients, 0)

    def sweep(p):
        join(st.at[p])

        def plane(y, carry):
            for i in range(TILES):
                at = row8(i)
                c = th[p, y + 1, tile(i)]
                south, north = span_neighbours(c, pz[at], y)
                new = (
                    (hb[y, at] + co[AD, y, at] * c)
                    + (co[AW, y, at] * th[p, y + 1, tile(i, -1)] + co[AE, y, at] * th[p, y + 1, tile(i, 1)])
                    + (co[AS, y, at] * south + co[AN, y, at] * north)
                    + (co[AB, y, at] * th[p, y, tile(i)] + co[AA, y, at] * th[p, y + 2, tile(i)])
                )
                th[1 - p, y + 1, tile(i)] = new
                if i == last:
                    th[1 - p, y + 1, tile(-1)] = new
                if i == 0:
                    th[1 - p, y + 1, tile(TILES)] = new
            return carry

        lax.fori_loop(0, CY, plane, 0)
        for side in range(2):
            for i in range(TILES):
                at = row8(i)
                c = st[p, side, tile(i)]
                below = jnp.where(group == 0, sw[side, at], pltpu.roll(c, 8, 1))
                a = [sco[slot, side, at] for slot in range(8)]
                new = (
                    (a[SRC] + a[AD] * c)
                    + (a[AW] * st[p, side, tile(i, -1)] + a[AE] * st[p, side, tile(i, 1)])
                    + (a[AS] * pltpu.roll(c, 1, 1) + a[AN] * pltpu.roll(c, LZ - 1, 1))
                    + (a[AB] * below + a[AA] * pltpu.roll(c, LZ - 8, 1))
                )
                st[1 - p, side, tile(i)] = new
                if i == last:
                    st[1 - p, side, tile(-1)] = new
                if i == 0:
                    st[1 - p, side, tile(TILES)] = new

    own = pl.ds(8, CX)

    def send_faces(r, p):
        field, wall = th[p, 1, own], th[p, 0, own]
        sent = fluid * (kb[0, own] * (field - wall)) + metal * field
        sb[...] = pick(choose_send[...], sent).reshape(n, chunk, LZ)

        def to(zd, i):
            x, y, c = (b // 4) % 4 + 3 - i // 4, (b // 2) % 2 + 1 - (i // 2) % 2, b % 2 + 1 - i % 2
            z = lax.rem(b // 16 + zd, n // 16)
            t = z * 16 + lax.rem(x, 4) * 4 + lax.rem(y, 2) * 2 + lax.rem(c, 2)
            remote(sb.at[t], rb.at[r, b], many_send.at[r], many_recv.at[r], (t, s)).start()

        for zd in (4, 3, 5, 2, 6, 1, 7):
            if zd < n // 16:
                lax.fori_loop(0, 16, lambda i, carry, zd=zd: (to(zd, i), carry)[1], 0)
        lax.fori_loop(0, 15, lambda i, carry: (to(0, i), carry)[1], 0)

    def receive_faces(r):
        others = pl.ds(0, n - 1)
        remote(sb.at[others], rb.at[r, others], many_send.at[r], many_recv.at[r], Z).wait()
        return pick(choose_recv[...], rb[r].reshape(2 * CX, LZ))

    p = 0
    for _ in range(SWEEPS):
        sweep(p)
        p = 1 - p
    send_faces(0, p)

    def pack_theta(i, carry):
        at_pad = pl.ds(pl.multiple_of(8 * i + 8, 8), 8)
        q1[pl.ds(pl.multiple_of(8 * i, 8), 8)] = edges(lambda y: th[p, y + 1, at_pad])
        return carry

    lax.fori_loop(0, TILES - 1, pack_theta, 0)
    planes = pl.ds(1, CY)
    copies = [
        remote(th.at[p, planes, pl.ds(CX, 8)], tr.at[0], send_sem.at[10], recv_sem.at[10], E),
        remote(th.at[p, planes, pl.ds(8, 8)], tr.at[1], send_sem.at[11], recv_sem.at[11], W),
        remote(q1.at[pl.ds(CX - 8, 8)], c1r.at[0], send_sem.at[12], recv_sem.at[12], ZE),
        remote(q1.at[pl.ds(0, 8)], c1r.at[1], send_sem.at[13], recv_sem.at[13], ZW),
        remote(q1, q1r, send_sem.at[14], recv_sem.at[14], Z),
    ]
    for copy in copies:
        copy.start()
    for copy in copies:
        copy.wait()

    def unpack_theta(y, carry):
        t = jnp.where(sub < 4, tr[1, y], tr[0, y])
        th[p, y + 1, tile(last)] = t
        th[p, y + 1, tile(-1)] = t
        return carry

    lax.fori_loop(0, CY, unpack_theta, 0)
    halo_th = edges(lambda y: th[p, y + 1, tile(last)])
    for i in range(TILES):
        own_q = q1[row8(i)] if i < last else halo_th
        other_q = q1r[row8(i)] if i < last else jnp.where(sub < 4, c1r[1], c1r[0])
        put_strip(st.at[p], i, own_q, other_q)

    th[p, 0, own] = receive_faces(0)
    copies = wall_copies(1, th.at[p, 0], 15)
    for copy in copies:
        copy.start()
    for copy in copies:
        copy.wait()
    strip_wall(1, p)
    for _ in range(SWEEPS):
        sweep(p)
        p = 1 - p
    send_faces(1, p)
    store = pltpu.make_async_copy(th.at[p, planes, own], theta_out.at[0], load_sem.at[0])
    store.start()
    wall_out[0] = receive_faces(1)
    store.wait()


def solution(mesh):
    n = mesh.shape["blk"]
    chunk = 2 * CX // n

    def part(theta, cond, vel, heat, wall, kinds, blocks, rows):
        hbm = pl.BlockSpec(memory_space=pl.ANY)
        vmem = pl.BlockSpec(memory_space=pltpu.VMEM)
        buf = lambda *shape: pltpu.VMEM(shape, F32)
        return pl.pallas_call(
            functools.partial(kernel, n),
            out_shape=(
                jax.ShapeDtypeStruct(theta.shape, F32),
                jax.ShapeDtypeStruct(wall.shape, F32),
            ),
            in_specs=[hbm] * 5 + [pl.BlockSpec(memory_space=pltpu.SMEM), vmem, vmem],
            out_specs=(hbm, vmem),
            scratch_shapes=[
                buf(2, CY + 2, PAD, LZ),
                buf(CY, PAD, LZ),
                buf(3, CY, ROWS, LZ),
                buf(CY, ROWS, LZ),
                buf(7, CY, ROWS, LZ),
                buf(2, 2, PAD, LZ),
                buf(2, PAD, LZ),
                buf(4, 2, ROWS, LZ),
                buf(8, 2, ROWS, LZ),
                buf(2, ROWS, LZ),
                buf(ROWS, LZ),
                buf(2, 2, CY, 8, LZ),
                buf(2, 2, CY, 8, LZ),
                buf(4, CX, LZ),
                buf(4, CX, LZ),
                buf(2, 4, 8, LZ),
                buf(2, 2, 8, LZ),
                buf(2, CX, LZ),
                buf(2, 2, 8, LZ),
                buf(2, CY, 8, LZ),
                buf(CX, LZ),
                buf(CX, LZ),
                buf(2, 8, LZ),
                buf(n, chunk, LZ),
                buf(2, n, chunk, LZ),
                pltpu.VMEM((2 * CX, CX), jnp.bfloat16),
                pltpu.VMEM((CX, 2 * CX), jnp.bfloat16),
                pltpu.SemaphoreType.DMA((5,)),
                pltpu.SemaphoreType.DMA((20,)),
                pltpu.SemaphoreType.DMA((20,)),
                pltpu.SemaphoreType.DMA((2,)),
                pltpu.SemaphoreType.DMA((2,)),
            ],
            compiler_params=pltpu.CompilerParams(
                collective_id=0, has_side_effects=True, vmem_limit_bytes=48 * 2**20
            ),
        )(theta, cond, vel, heat, wall, kinds, blocks, rows)

    whole = P("blk", None, None, "span")
    rows = P("blk", None, "span")
    return jax.shard_map(
        part,
        mesh=mesh,
        in_specs=(whole, whole, P("blk", None, None, None, "span"), whole, rows, P(), P("blk", None), P("blk", None)),
        out_specs=(whole, rows),
        check_vma=False,
    )
```

```python
import functools

import jax
import jax.numpy as jnp
from jax import lax
from jax.experimental import pallas as pl
from jax.experimental.pallas import tpu as pltpu
from jax.sharding import PartitionSpec as P

MESH = pl.DeviceIdType.MESH
ITERS, SWEEPS = 2, 3
CY, CX, LZ = 16, 128, 128
TILES = CX // 8 + 1
ROWS = 8 * TILES
PAD = ROWS + 16
F32 = jnp.float32
AW, AE, AS, AN, AB, AA, AD, SRC = range(8)


def tile(i, shift=0):
    return pl.ds(8 + 8 * i + shift, 8)


def row8(i):
    return pl.ds(8 * i, 8)


def remote(src, dst, send, recv, device):
    return pltpu.make_async_remote_copy(
        src_ref=src, dst_ref=dst, send_sem=send, recv_sem=recv, device_id=device, device_id_type=MESH
    )


def split3(x):
    hi = x.astype(jnp.bfloat16)
    rest = x - hi.astype(F32)
    mid = rest.astype(jnp.bfloat16)
    low = (rest - mid.astype(F32)).astype(jnp.bfloat16)
    return hi, mid, low


def pick(chooser, x):
    return sum(jnp.dot(chooser, part, preferred_element_type=F32) for part in split3(x))


def kernel(
    n, theta_ref, cond_ref, vel_ref, heat_ref, wall_ref, kind_ref, block_ref, row_ref,
    theta_out, wall_out,
    th, kb, vb, hb, co, st, sk, sv, sco, sw, pz,
    xs, xr, qo, qs, qr, cr, qt, qtr, ct, wx, wp, wc, tr,
    sb, rb, choose_send, choose_recv, kinds, blocks, rows,
    load_sem, send_sem, recv_sem, wall_send, wall_recv, theta_send, theta_recv, many_send, many_recv,
):
    b, s = lax.axis_index("blk"), lax.axis_index("span")
    chunk = 2 * CX // n
    east, west = lax.rem(b + 1, n), lax.rem(b + n - 1, n)
    E, W, Z, ZE, ZW = (east, s), (west, s), (b, 1 - s), (east, 1 - s), (west, 1 - s)
    own, planes = pl.ds(8, CX), pl.ds(1, CY)

    loads = [
        pltpu.make_async_copy(kind_ref, kinds, load_sem.at[5]),
        pltpu.make_async_copy(block_ref, blocks, load_sem.at[6]),
        pltpu.make_async_copy(row_ref, rows, load_sem.at[7]),
        pltpu.make_async_copy(theta_ref.at[0], th.at[0, planes, own], load_sem.at[0]),
        pltpu.make_async_copy(cond_ref.at[0], kb.at[:, own], load_sem.at[1]),
        pltpu.make_async_copy(vel_ref.at[0], vb.at[:, :, pl.ds(0, CX)], load_sem.at[2]),
        pltpu.make_async_copy(heat_ref.at[0], hb.at[:, pl.ds(0, CX)], load_sem.at[3]),
        pltpu.make_async_copy(wall_ref.at[0], th.at[0, 0, own], load_sem.at[4]),
    ]
    for load in loads:
        load.start()

    rb[:, pl.ds(b, 1)] = jnp.zeros((2, 1, chunk, LZ), F32)

    barrier = pltpu.get_barrier_semaphore()

    def greet(d, carry):
        pl.semaphore_signal(barrier, inc=1, device_id=(lax.rem(b + d, n), s), device_id_type=MESH)
        return carry

    lax.fori_loop(1, n, greet, 0)
    for peer in (Z, ZE, ZW):
        pl.semaphore_signal(barrier, inc=1, device_id=peer, device_id_type=MESH)

    lane = lax.broadcasted_iota(jnp.int32, (8, LZ), 1)
    sub = lax.broadcasted_iota(jnp.int32, (8, LZ), 0)
    group, place = lane // 8, lane % 8
    first_lane, last_lane = lane == 0, lane == LZ - 1
    low_half = place < 4
    middle = (place >= 2) & (place < 6)
    near = sub < 4
    last = TILES - 1

    for t in range(4):
        th[t, CY + 1] = jnp.zeros((PAD, LZ), F32)

    for load in loads:
        load.wait()
    fluid = kinds[b].astype(F32)
    metal = 1.0 - fluid
    same_west = 1.0 - jnp.abs(kinds[west].astype(F32) - fluid)
    same_east = 1.0 - jnp.abs(kinds[east].astype(F32) - fluid)

    def edges(load):
        out = pltpu.roll(load(0), 4, 1)
        for y in range(1, CY):
            out = jnp.where(group == y, pltpu.roll(load(y), (8 * y + 4) % LZ, 1), out)
        return out

    def pack_static(at, at_pad):
        q_k = edges(lambda y: kb[y, at_pad])
        q_v = [edges(lambda y, d=d: vb[d, y, at]) for d in range(3)]
        q_h = edges(lambda y: hb[y, at])
        return [q_k] + q_v + [q_h]

    def paired(q):
        return [
            q[0],
            jnp.where(middle, q[1], pltpu.roll(q[2], 4, 1)),
            jnp.where(middle, q[3], pltpu.roll(q[4], 4, 1)),
        ]

    def pack_tile(i, carry):
        at = pl.ds(pl.multiple_of(8 * i, 8), 8)
        at_pad = pl.ds(pl.multiple_of(8 * i + 8, 8), 8)
        q_th, q_static = edges(lambda y: th[0, y + 1, at_pad]), pack_static(at, at_pad)
        qt[0, at] = q_th
        for slot, q in enumerate(q_static):
            qo[slot, at] = q
        for slot, q in enumerate(paired(q_static)):
            qs[slot, at] = q
        return carry

    lax.fori_loop(0, TILES - 1, pack_tile, 0, unroll=2)

    def pack_rows(y, carry):
        end, pad_end = pl.ds(CX - 8, 8), pl.ds(CX, 8)
        xs[0, 0, y] = jnp.where(sub >= 5, th[0, y + 1, pad_end], pltpu.roll(kb[y, pad_end], 5, 0))
        xs[0, 1, y] = jnp.where(
            sub >= 6,
            vb[0, y, end],
            jnp.where(
                sub >= 4,
                pltpu.roll(vb[1, y, end], 6, 0),
                jnp.where(sub >= 2, pltpu.roll(vb[2, y, end], 4, 0), pltpu.roll(hb[y, end], 2, 0)),
            ),
        )
        zero, pad_zero = pl.ds(0, 8), pl.ds(8, 8)
        xs[1, 0, y] = jnp.where(sub < 3, th[0, y + 1, pad_zero], pltpu.roll(kb[y, pad_zero], 3, 0))
        xs[1, 1, y] = jnp.where(
            sub < 2,
            vb[0, y, zero],
            jnp.where(
                sub < 4,
                pltpu.roll(vb[1, y, zero], 2, 0),
                jnp.where(sub < 6, pltpu.roll(vb[2, y, zero], 4, 0), pltpu.roll(hb[y, zero], 6, 0)),
            ),
        )
        return carry

    lax.fori_loop(0, CY, pack_rows, 0, unroll=4)

    pl.semaphore_wait(barrier, n + 2)

    def wall_copies(r, t):
        plane, ss, rs = th.at[t, 0], wall_send.at[r], wall_recv.at[r]
        tail, head = plane.at[pl.ds(CX, 8)], plane.at[pl.ds(8, 8)]
        return [
            remote(tail, wx.at[r, 0], ss.at[0], rs.at[0], E),
            remote(head, wx.at[r, 1], ss.at[1], rs.at[1], W),
            remote(tail, wc.at[r, 0], ss.at[3], rs.at[3], ZE),
            remote(head, wc.at[r, 1], ss.at[4], rs.at[4], ZW),
            remote(plane.at[own], wp.at[r], ss.at[2], rs.at[2], Z),
        ]

    def theta_strip_copies(r):
        q, ss, rs = qt.at[r], theta_send.at[r], theta_recv.at[r]
        return [
            remote(q.at[pl.ds(CX - 8, 8)], ct.at[r, 0], ss.at[1], rs.at[1], ZE),
            remote(q.at[pl.ds(0, 8)], ct.at[r, 1], ss.at[2], rs.at[2], ZW),
            remote(q, qtr.at[r], ss.at[0], rs.at[0], Z),
        ]

    theta_copies = [
        remote(th.at[3, planes, pl.ds(CX, 8)], tr.at[0], theta_send.at[1, 3], theta_recv.at[1, 3], E),
        remote(th.at[3, planes, pl.ds(8, 8)], tr.at[1], theta_send.at[1, 4], theta_recv.at[1, 4], W),
    ]
    static_copies = [
        remote(xs.at[0], xr.at[0], send_sem.at[0], recv_sem.at[0], E),
        remote(xs.at[1], xr.at[1], send_sem.at[1], recv_sem.at[1], W),
        remote(qs.at[:, pl.ds(CX - 8, 8)], cr.at[0], send_sem.at[3], recv_sem.at[3], ZE),
        remote(qs.at[:, pl.ds(0, 8)], cr.at[1], send_sem.at[4], recv_sem.at[4], ZW),
        remote(qs, qr, send_sem.at[2], recv_sem.at[2], Z),
    ]
    for copy in static_copies + theta_strip_copies(0) + wall_copies(0, 0):
        copy.start()

    mine = jnp.broadcast_to(blocks[...].astype(F32), (CX, CX))
    theirs = jnp.broadcast_to(rows[...].astype(F32), (CX, CX))
    mine_t, theirs_t = mine.T, theirs.T
    at_row = lax.broadcasted_iota(jnp.int32, (CX, CX), 0)
    at_col = lax.broadcasted_iota(jnp.int32, (CX, CX), 1)
    alike = mine_t == mine
    rank = jnp.sum(jnp.where(alike & (at_row < at_col), 1.0, 0.0), axis=0, keepdims=True)
    code = (chunk * mine[0:1] + rank).astype(jnp.int32)
    choose_send[...] = jnp.where(
        lax.broadcasted_iota(jnp.int32, (2 * CX, CX), 0) == code, 1.0, 0.0
    ).astype(jnp.bfloat16)
    rank_t = jnp.sum(jnp.where(alike & (theirs < theirs_t), 1.0, 0.0), axis=1, keepdims=True)
    code_t = (chunk * mine_t[:, 0:1] + rank_t).astype(jnp.int32)
    choose_recv[...] = jnp.where(
        lax.broadcasted_iota(jnp.int32, (CX, 2 * CX), 1) == code_t, 1.0, 0.0
    ).astype(jnp.bfloat16)

    for copy in static_copies:
        copy.wait()

    rows_last = row8(last)

    def unpack_rows(y, carry):
        e0, e1, w0, w1 = xr[1, 0, y], xr[1, 1, y], xr[0, 0, y], xr[0, 1, y]
        t = jnp.where(near, e0, w0)
        th[0, y + 1, tile(last)] = t
        th[0, y + 1, tile(-1)] = t
        th[0, y + 1, tile(TILES)] = th[0, y + 1, tile(0)]
        k = jnp.where(near, pltpu.roll(e0, 5, 0), pltpu.roll(w0, 3, 0))
        kb[y, tile(last)] = k
        kb[y, tile(-1)] = k
        kb[y, tile(TILES)] = kb[y, tile(0)]
        vb[0, y, rows_last] = jnp.where(near, e1, w1)
        vb[1, y, rows_last] = jnp.where(near, pltpu.roll(e1, 6, 0), pltpu.roll(w1, 2, 0))
        vb[2, y, rows_last] = jnp.where(near, pltpu.roll(e1, 4, 0), pltpu.roll(w1, 4, 0))
        hb[y, rows_last] = jnp.where(near, pltpu.roll(e1, 2, 0), pltpu.roll(w1, 6, 0))
        return carry

    lax.fori_loop(0, CY, unpack_rows, 0, unroll=4)

    def put_strip(ref, at, own_q, other_q):
        ref[0, at] = jnp.where(low_half, other_q, own_q)
        ref[1, at] = jnp.where(low_half, own_q, other_q)

    def put_static(at, at_pad, own_q, other_q):
        put_strip(sk, at_pad, own_q[0], other_q[0])
        for slot in range(2):
            t = other_q[1 + slot]
            put_strip(sv.at[2 * slot], at, own_q[1 + 2 * slot], t)
            put_strip(sv.at[2 * slot + 1], at, own_q[2 + 2 * slot], pltpu.roll(t, LZ - 4, 1))

    def static_strip(i, carry):
        at = pl.ds(pl.multiple_of(8 * i, 8), 8)
        at_pad = pl.ds(pl.multiple_of(8 * i + 8, 8), 8)
        put_static(at, at_pad, [qo[slot, at] for slot in range(5)], [qr[slot, at] for slot in range(3)])
        return carry

    lax.fori_loop(0, TILES - 1, static_strip, 0, unroll=4)
    put_static(
        rows_last, tile(last), pack_static(rows_last, tile(last)),
        [jnp.where(near, cr[1, slot], cr[0, slot]) for slot in range(3)],
    )

    def wrap(ref):
        for side in range(2):
            ref[side, tile(-1)] = ref[side, tile(last)]
            ref[side, tile(TILES)] = ref[side, tile(0)]

    wrap(sk)

    def coefficients(k, k_w, k_e, k_s, k_n, k_b, k_a, v, mask_w, mask_e, bottom, top):
        v = [fluid * x for x in v]
        a_w = mask_w(0.5 * (k + k_w) + jnp.maximum(v[0], 0.0))
        a_e = mask_e(0.5 * (k + k_e) - jnp.minimum(v[0], 0.0))
        a_b = 0.5 * (k + k_b) + jnp.maximum(v[1], 0.0)
        a_b = a_b * (1.0 - metal * bottom)
        a_a = (0.5 * (k + k_a) - jnp.minimum(v[1], 0.0)) * (1.0 - top)
        a_s = 0.5 * (k + k_s) + jnp.maximum(v[2], 0.0)
        a_n = 0.5 * (k + k_n) - jnp.minimum(v[2], 0.0)
        a_d = 1.0 - (a_w + a_e + a_s + a_n + a_b + a_a)
        return a_w, a_e, a_s, a_n, a_b + metal * bottom, a_a, a_d

    whole, whole_w, whole_e = pl.ds(8, ROWS), pl.ds(7, ROWS), pl.ds(9, ROWS)
    strip_row = lax.broadcasted_iota(jnp.int32, (ROWS, LZ), 0)
    strip_group = lax.broadcasted_iota(jnp.int32, (ROWS, LZ), 1) // 8
    strip_first = strip_group == 0

    def strip_coefficients(side, carry):
        k = sk[side, whole]
        a = coefficients(
            k, sk[side, whole_w], sk[side, whole_e], pltpu.roll(k, 1, 1), pltpu.roll(k, LZ - 1, 1),
            jnp.where(strip_first, k, pltpu.roll(k, 8, 1)), pltpu.roll(k, LZ - 8, 1), [sv[d, side] for d in range(3)],
            lambda x: jnp.where(strip_row == 0, same_west * x, x),
            lambda x: jnp.where(strip_row == CX - 1, same_east * x, x),
            strip_first.astype(F32), (strip_group == CY - 1).astype(F32),
        )
        for slot, value in enumerate(a):
            sco[slot, side] = value
        return carry

    lax.fori_loop(0, 2, strip_coefficients, 0)
    def plane_coefficients(y, carry):
        bottom = (y == 0).astype(F32)
        top = (y == CY - 1).astype(F32)
        below, above = jnp.maximum(y - 1, 0), jnp.minimum(y + 1, CY - 1)
        for i in range(TILES):
            k = kb[y, tile(i)]
            k_s, k_n = pltpu.roll(k, 1, 1), pltpu.roll(k, LZ - 1, 1)
            mask_w = (lambda x: jnp.where(sub == 0, same_west * x, x)) if i == 0 else (lambda x: x)
            mask_e = (lambda x: jnp.where(sub == 7, same_east * x, x)) if i == last - 1 else (lambda x: x)
            a = coefficients(
                k, kb[y, tile(i, -1)], kb[y, tile(i, 1)], k_s, k_n, kb[below, tile(i)], kb[above, tile(i)],
                [vb[d, y, row8(i)] for d in range(3)], mask_w, mask_e, bottom, top,
            )
            for slot, value in enumerate(a):
                co[slot, y, row8(i)] = value
        return carry

    edge_two, edge_one = (lane < 2) | (lane >= LZ - 2), first_lane | last_lane

    def sweep(t, following, step, first, end):
        def pair(g, carry):
            for half in range(2):
                y = 2 * g + half
                for i in range(TILES):
                    at = row8(i)
                    c = th[t, y + 1, tile(i)]
                    new = (
                        (hb[y, at] + co[AD, y, at] * c)
                        + (co[AW, y, at] * th[t, y + 1, tile(i, -1)] + co[AE, y, at] * th[t, y + 1, tile(i, 1)])
                        + (co[AS, y, at] * pltpu.roll(c, 1, 1) + co[AN, y, at] * pltpu.roll(c, LZ - 1, 1))
                        + (co[AB, y, at] * th[t, y, tile(i)] + co[AA, y, at] * th[t, y + 2, tile(i)])
                    )
                    if step > 0:
                        new = jnp.where(edge_two if step == 1 else edge_one, pz[step - 1, y, at], new)
                    th[following, y + 1, tile(i)] = new
                    if i == last:
                        th[following, y + 1, tile(-1)] = new
                    if i == 0:
                        th[following, y + 1, tile(TILES)] = new
            return carry

        lax.fori_loop(first, end, pair, 0)

    def strip_sweep(m, carry):
        step, side = m // 2, m % 2
        c = st[step, side, whole]
        below = jnp.where(strip_first, sw[side], pltpu.roll(c, 8, 1))
        new = (
            (sv[3, side] + sco[AD, side] * c)
            + (sco[AW, side] * st[step, side, whole_w] + sco[AE, side] * st[step, side, whole_e])
            + (sco[AS, side] * pltpu.roll(c, 1, 1) + sco[AN, side] * pltpu.roll(c, LZ - 1, 1))
            + (sco[AB, side] * below + sco[AA, side] * pltpu.roll(c, LZ - 8, 1))
        )
        st[step + 1, side, whole] = new
        st[step + 1, side, tile(-1)] = new[ROWS - 8 :]
        st[step + 1, side, tile(TILES)] = new[:8]
        return carry

    def spread(slot, first, end):
        strips = [jnp.where(low_half, st[slot + 2, 1, tile(i)], st[slot + 2, 0, tile(i)]) for i in range(TILES)]
        for y in range(first, end):
            for i in range(TILES):
                pz[slot, y, row8(i)] = pltpu.roll(strips[i], 124 - 8 * y, 1)

    def send_faces(r, t):
        field, wall = th[t, 1, own], th[t, 0, own]
        sent = fluid * (kb[0, own] * (field - wall)) + metal * field
        sb[...] = pick(choose_send[...], sent).reshape(n, chunk, LZ)

        def to(zd, i):
            x, y, c = (b // 4) % 4 + 3 - i // 4, (b // 2) % 2 + 1 - (i // 2) % 2, b % 2 + 1 - i % 2
            z = lax.rem(b // 16 + zd, n // 16)
            t = z * 16 + lax.rem(x, 4) * 4 + lax.rem(y, 2) * 2 + lax.rem(c, 2)
            remote(sb.at[t], rb.at[r, b], many_send.at[r], many_recv.at[r], (t, s)).start()

        for zd in (4, 3, 5, 2, 6, 1, 7):
            if zd < n // 16:
                lax.fori_loop(0, 16, lambda i, carry, zd=zd: (to(zd, i), carry)[1], 0, unroll=2)
        lax.fori_loop(0, 15, lambda i, carry: (to(0, i), carry)[1], 0, unroll=3)

    def receive_faces(r):
        others = pl.ds(0, n - 1)
        remote(sb.at[others], rb.at[r, others], many_send.at[r], many_recv.at[r], Z).wait()
        return pick(choose_recv[...], rb[r].reshape(2 * CX, LZ))

    def theta_strip(r):
        def one(i, carry):
            at = pl.ds(pl.multiple_of(8 * i, 8), 8)
            at_pad = pl.ds(pl.multiple_of(8 * i + 8, 8), 8)
            put_strip(st.at[0], at_pad, qt[r, at], qtr[r, at])
            own_w = pltpu.roll(th[3 * r, 0, at_pad], 4, 1)
            put_strip(sw, at, own_w, pltpu.roll(wp[r, at], 4, 1))
            return carry

        lax.fori_loop(0, TILES - 1, one, 0, unroll=4)
        put_strip(
            st.at[0], tile(last), edges(lambda y: th[3 * r, y + 1, tile(last)]), jnp.where(near, ct[r, 1], ct[r, 0])
        )
        wrap(st.at[0])
        wall_last = jnp.where(near, wx[r, 1], wx[r, 0])
        th[3 * r, 0, tile(last)] = wall_last
        put_strip(
            sw, rows_last, pltpu.roll(wall_last, 4, 1), pltpu.roll(jnp.where(near, wc[r, 1], wc[r, 0]), 4, 1)
        )
        wall = th[3 * r, 0, whole]
        for t in range(4):
            th[t, 0, whole] = wall

    def unpack_theta(y, carry):
        t = jnp.where(near, tr[1, y], tr[0, y])
        th[3, y + 1, tile(last)] = t
        th[3, y + 1, tile(-1)] = t
        return carry

    def pack_theta(i, carry):
        at_pad = pl.ds(pl.multiple_of(8 * i + 8, 8), 8)
        qt[1, pl.ds(pl.multiple_of(8 * i, 8), 8)] = edges(lambda y: th[3, y + 1, at_pad])
        return carry

    store = pltpu.make_async_copy(th.at[2, planes, own], theta_out.at[0], load_sem.at[0])

    def iteration(r):
        for copy in theta_strip_copies(r) + wall_copies(r, 3 * r):
            copy.wait()
        if r == 1:
            for copy in theta_copies:
                copy.wait()
            lax.fori_loop(0, CY, unpack_theta, 0, unroll=4)
        theta_strip(r)
        lax.fori_loop(0, 2 * SWEEPS, strip_sweep, 0)

        def phase(late, carry):
            for slot in range(2):

                @pl.when(late == 0)
                def _():
                    spread(slot, 0, 4)

                @pl.when(late == 1)
                def _():
                    spread(slot, 4, CY)

            if r == 0:
                lax.fori_loop(4 * late, 4 + (CY - 4) * late, plane_coefficients, 0)
            for step in range(SWEEPS):
                sweep(
                    (3 * r + step) % 4, (3 * r + step + 1) % 4, step,
                    late * (2 - step), (1 - late) * max(2 - step, 1) + late * (CY // 2),
                )

            @pl.when(late == 0)
            def _():
                send_faces(r, (3 * r + 3) % 4)

            return carry

        lax.fori_loop(0, 2, phase, 0)
        if r == 0:
            lax.fori_loop(0, TILES - 1, pack_theta, 0, unroll=4)
            for copy in theta_copies + theta_strip_copies(1):
                copy.start()
        else:
            store.start()
        th[3 - r, 0, own] = receive_faces(r)
        if r == 0:
            for copy in wall_copies(1, 3):
                copy.start()

    for r in range(ITERS):
        iteration(r)
    wall_out[0] = th[2, 0, own]
    store.wait()


def solution(mesh):
    n = mesh.shape["blk"]
    chunk = 2 * CX // n

    def part(theta, cond, vel, heat, wall, kinds, blocks, rows):
        hbm = pl.BlockSpec(memory_space=pltpu.HBM)
        anywhere = pl.BlockSpec(memory_space=pl.ANY)
        vmem = pl.BlockSpec(memory_space=pltpu.VMEM)
        buf = lambda *shape: pltpu.VMEM(shape, F32)
        return pl.pallas_call(
            functools.partial(kernel, n),
            out_shape=(
                jax.ShapeDtypeStruct(theta.shape, F32),
                jax.ShapeDtypeStruct(wall.shape, F32),
            ),
            in_specs=[hbm] * 8,
            out_specs=(anywhere, vmem),
            scratch_shapes=[
                buf(4, CY + 2, PAD, LZ),
                buf(CY, PAD, LZ),
                buf(3, CY, ROWS, LZ),
                buf(CY, ROWS, LZ),
                buf(7, CY, ROWS, LZ),
                buf(4, 2, PAD, LZ),
                buf(2, PAD, LZ),
                buf(4, 2, ROWS, LZ),
                buf(7, 2, ROWS, LZ),
                buf(2, ROWS, LZ),
                buf(2, CY, ROWS, LZ),
                buf(2, 2, CY, 8, LZ),
                buf(2, 2, CY, 8, LZ),
                buf(5, CX, LZ),
                buf(3, CX, LZ),
                buf(3, CX, LZ),
                buf(2, 3, 8, LZ),
                buf(2, CX, LZ),
                buf(2, CX, LZ),
                buf(2, 2, 8, LZ),
                buf(2, 2, 8, LZ),
                buf(2, CX, LZ),
                buf(2, 2, 8, LZ),
                buf(2, CY, 8, LZ),
                buf(n, chunk, LZ),
                buf(2, n, chunk, LZ),
                pltpu.VMEM((2 * CX, CX), jnp.bfloat16),
                pltpu.VMEM((CX, 2 * CX), jnp.bfloat16),
                pltpu.SMEM((n,), jnp.int32),
                pltpu.VMEM((1, CX), jnp.int32),
                pltpu.VMEM((1, CX), jnp.int32),
                pltpu.SemaphoreType.DMA((8,)),
                pltpu.SemaphoreType.DMA((5,)),
                pltpu.SemaphoreType.DMA((5,)),
                pltpu.SemaphoreType.DMA((2, 5)),
                pltpu.SemaphoreType.DMA((2, 5)),
                pltpu.SemaphoreType.DMA((2, 5)),
                pltpu.SemaphoreType.DMA((2, 5)),
                pltpu.SemaphoreType.DMA((2,)),
                pltpu.SemaphoreType.DMA((2,)),
            ],
            compiler_params=pltpu.CompilerParams(
                collective_id=0, has_side_effects=True, vmem_limit_bytes=56 * 2**20
            ),
        )(theta, cond, vel, heat, wall, kinds, blocks, rows)

    whole = P("blk", None, None, "span")
    rows = P("blk", None, "span")
    return jax.shard_map(
        part,
        mesh=mesh,
        in_specs=(whole, whole, P("blk", None, None, None, "span"), whole, rows, P(), P("blk", None), P("blk", None)),
        out_specs=(whole, rows),
        check_vma=False,
    )
```

```python
import functools

import jax
import jax.numpy as jnp
from jax import lax
from jax.experimental import pallas as pl
from jax.experimental.pallas import tpu as pltpu
from jax.sharding import PartitionSpec as P

MESH = pl.DeviceIdType.MESH
ITERS, SWEEPS = 2, 3
CY, CX, LZ = 16, 128, 128
LOW = 4
TILES = CX // 8 + 1
ROWS = 8 * TILES
PAD = ROWS + 16
F32 = jnp.float32
AW, AE, AS, AN, AB, AA, AD, SRC = range(8)


def tile(i, shift=0):
    return pl.ds(8 + 8 * i + shift, 8)


def row8(i):
    return pl.ds(8 * i, 8)


def remote(src, dst, send, recv, device):
    return pltpu.make_async_remote_copy(
        src_ref=src, dst_ref=dst, send_sem=send, recv_sem=recv, device_id=device, device_id_type=MESH
    )


def split3(x):
    hi = x.astype(jnp.bfloat16)
    rest = x - hi.astype(F32)
    mid = rest.astype(jnp.bfloat16)
    low = (rest - mid.astype(F32)).astype(jnp.bfloat16)
    return hi, mid, low


def pick(chooser, x):
    return sum(jnp.dot(chooser, part, preferred_element_type=F32) for part in split3(x))


def kernel(
    n, theta_ref, cond_ref, vel_ref, heat_ref, wall_ref, kind_ref, block_ref, row_ref,
    theta_out, wall_out,
    th, kb, vb, hb, co, st, sk, sv, sco, sw, pz,
    xs, xr, qo, qs, qr, cr, qx, cx, qa, qar, ca, qt, qtr, ct, qw, qwr, wx, wc, tr,
    sb, rb, choose_send, choose_recv, kinds, blocks, rows,
    load_sem, low_send, low_recv, mid_send, mid_recv, rest_send, rest_recv, wall_send, wall_recv, theta_send, theta_recv,
    many_send, many_recv, known,
):
    b, s = lax.axis_index("blk"), lax.axis_index("span")
    chunk = 2 * CX // n
    east, west = lax.rem(b + 1, n), lax.rem(b + n - 1, n)
    E, W, Z, ZE, ZW = (east, s), (west, s), (b, 1 - s), (east, 1 - s), (west, 1 - s)
    own, planes = pl.ds(8, CX), pl.ds(1, CY)

    loads = [
        pltpu.make_async_copy(kind_ref, kinds, load_sem.at[5]),
        pltpu.make_async_copy(block_ref, blocks, load_sem.at[6]),
        pltpu.make_async_copy(row_ref, rows, load_sem.at[7]),
        pltpu.make_async_copy(theta_ref.at[0], th.at[0, planes, own], load_sem.at[0]),
        pltpu.make_async_copy(cond_ref.at[0], kb.at[:, own], load_sem.at[1]),
        pltpu.make_async_copy(vel_ref.at[0], vb.at[:, :, pl.ds(0, CX)], load_sem.at[2]),
        pltpu.make_async_copy(heat_ref.at[0], hb.at[:, pl.ds(0, CX)], load_sem.at[3]),
        pltpu.make_async_copy(wall_ref.at[0], th.at[0, 0, own], load_sem.at[4]),
    ]
    for load in loads:
        load.start()

    rb[:, pl.ds(b, 1)] = jnp.zeros((2, 1, chunk, LZ), F32)

    def line(count, stride):
        at = lax.rem(b // stride, count)
        return [(b + (lax.rem(at + d, count) - at) * stride, s) for d in range(1, count)]

    line_z, line_x, line_y = line(n // 16, 16), line(4, 4), line(4, 1)
    barrier = pltpu.get_barrier_semaphore()
    beside = [E, W, Z, ZE, ZW] + line_z + line_x + line_y
    for peer in beside:
        pl.semaphore_signal(barrier, inc=1, device_id=peer, device_id_type=MESH)

    lane = lax.broadcasted_iota(jnp.int32, (8, LZ), 1)
    sub = lax.broadcasted_iota(jnp.int32, (8, LZ), 0)
    group, place = lane // 8, lane % 8
    first_lane, last_lane = lane == 0, lane == LZ - 1
    low_half = place < 4
    middle = (place >= 2) & (place < 6)
    near = sub < 4
    last = TILES - 1

    for t in range(4):
        th[t, CY + 1] = jnp.zeros((PAD, LZ), F32)

    for load in loads:
        load.wait()
    fluid = kinds[b].astype(F32)
    metal = 1.0 - fluid
    same_west = 1.0 - jnp.abs(kinds[west].astype(F32) - fluid)
    same_east = 1.0 - jnp.abs(kinds[east].astype(F32) - fluid)

    def edges(load, count=CY):
        out = pltpu.roll(load(0), 4, 1)
        for y in range(1, count):
            out = jnp.where(group == y, pltpu.roll(load(y), (8 * y + 4) % LZ, 1), out)
        return out

    def pack_static(at, at_pad):
        q_k = edges(lambda y: kb[y, at_pad])
        q_v = [edges(lambda y, d=d: vb[d, y, at]) for d in range(3)]
        q_h = edges(lambda y: hb[y, at])
        return [q_k] + q_v + [q_h]

    def paired(q):
        return [
            q[0],
            jnp.where(middle, q[1], pltpu.roll(q[2], 4, 1)),
            jnp.where(middle, q[3], pltpu.roll(q[4], 4, 1)),
        ]

    def pack_tile(i, carry):
        at = pl.ds(pl.multiple_of(8 * i, 8), 8)
        at_pad = pl.ds(pl.multiple_of(8 * i + 8, 8), 8)
        q = pack_static(at, at_pad) + [edges(lambda y: th[0, y + 1, at_pad])]
        sent = [q[5]] + paired(q)
        for slot in range(6):
            qo[slot, at] = q[slot]
        for slot in range(2):
            qs[slot, at] = jnp.where(group < 8, pltpu.roll(sent[2 * slot], 64, 1), sent[2 * slot + 1])
        for half in range(2):
            parts = [pltpu.roll(q, (32 * (slot - half)) % LZ, 1) if slot != half else q for slot, q in enumerate(sent)]
            out = parts[0]
            for slot in range(1, 4):
                out = jnp.where(group >= 4 * slot, parts[slot], out)
            qa[half, at] = out
        return carry

    lax.fori_loop(0, TILES - 1, pack_tile, 0, unroll=2)

    def pack_rows(y, carry):
        end, pad_end = pl.ds(CX - 8, 8), pl.ds(CX, 8)
        xs[0, 0, y] = jnp.where(sub >= 5, th[0, y + 1, pad_end], pltpu.roll(kb[y, pad_end], 5, 0))
        xs[0, 1, y] = jnp.where(
            sub >= 6,
            vb[0, y, end],
            jnp.where(
                sub >= 4,
                pltpu.roll(vb[1, y, end], 6, 0),
                jnp.where(sub >= 2, pltpu.roll(vb[2, y, end], 4, 0), pltpu.roll(hb[y, end], 2, 0)),
            ),
        )
        zero, pad_zero = pl.ds(0, 8), pl.ds(8, 8)
        xs[1, 0, y] = jnp.where(sub < 3, th[0, y + 1, pad_zero], pltpu.roll(kb[y, pad_zero], 3, 0))
        xs[1, 1, y] = jnp.where(
            sub < 2,
            vb[0, y, zero],
            jnp.where(
                sub < 4,
                pltpu.roll(vb[1, y, zero], 2, 0),
                jnp.where(sub < 6, pltpu.roll(vb[2, y, zero], 4, 0), pltpu.roll(hb[y, zero], 6, 0)),
            ),
        )
        return carry

    lax.fori_loop(0, CY, pack_rows, 0, unroll=4)

    def pack_wall(r, t):
        out = pltpu.roll(th[t, 0, tile(0)], 4, 1)
        for i in range(1, TILES - 1):
            out = jnp.where(group == i, pltpu.roll(th[t, 0, tile(i)], (8 * i + 4) % LZ, 1), out)
        qw[r] = out

    pack_wall(0, 0)

    pl.semaphore_wait(barrier, len(beside))
    for peer in line_x:
        pl.semaphore_signal(known.at[0], inc=1, device_id=peer, device_id_type=MESH)

    def wall_copies(r, t):
        plane, ss, rs = th.at[t, 0], wall_send.at[r], wall_recv.at[r]
        tail, head = plane.at[pl.ds(CX, 8)], plane.at[pl.ds(8, 8)]
        return [
            remote(tail, wc.at[r, 0], ss.at[3], rs.at[3], ZE),
            remote(head, wc.at[r, 1], ss.at[4], rs.at[4], ZW),
            remote(tail, wx.at[r, 0], ss.at[0], rs.at[0], E),
            remote(head, wx.at[r, 1], ss.at[1], rs.at[1], W),
            remote(qw.at[r], qwr.at[r], ss.at[2], rs.at[2], Z),
        ]

    head, tail = pl.ds(0, 8), pl.ds(CX - 8, 8)
    low, mid, rest = pl.ds(0, LOW), pl.ds(LOW, LOW), pl.ds(2 * LOW, CY - 2 * LOW)

    def theta_copies(late):
        ss, rs = theta_send.at[late], theta_recv.at[late]
        at, to = (pl.ds(1 + LOW, CY - LOW), pl.ds(LOW, CY - LOW)) if late else (pl.ds(1, LOW), low)
        return [
            remote(qt.at[late, tail], ct.at[late, 0], ss.at[1], rs.at[1], ZE),
            remote(qt.at[late, head], ct.at[late, 1], ss.at[2], rs.at[2], ZW),
            remote(th.at[3, at, pl.ds(CX, 8)], tr.at[0, to], ss.at[3], rs.at[3], E),
            remote(th.at[3, at, pl.ds(8, 8)], tr.at[1, to], ss.at[4], rs.at[4], W),
            remote(qt.at[late], qtr.at[late], ss.at[0], rs.at[0], Z),
        ]

    def part_copies(half, planes, ss, rs):
        return [
            remote(qa.at[half, tail], ca.at[half, 0], ss.at[3], rs.at[3], ZE),
            remote(qa.at[half, head], ca.at[half, 1], ss.at[4], rs.at[4], ZW),
            remote(xs.at[0, :, planes], xr.at[0, :, planes], ss.at[0], rs.at[0], E),
            remote(xs.at[1, :, planes], xr.at[1, :, planes], ss.at[1], rs.at[1], W),
            remote(qa.at[half], qar.at[half], ss.at[2], rs.at[2], Z),
        ]

    low_copies = part_copies(0, low, low_send, low_recv)
    mid_copies = part_copies(1, mid, mid_send, mid_recv)
    rest_copies = [
        remote(qs.at[:, tail], cr.at[0], rest_send.at[3], rest_recv.at[3], ZE),
        remote(qs.at[:, head], cr.at[1], rest_send.at[4], rest_recv.at[4], ZW),
        remote(xs.at[0, :, rest], xr.at[0, :, rest], rest_send.at[0], rest_recv.at[0], E),
        remote(xs.at[1, :, rest], xr.at[1, :, rest], rest_send.at[1], rest_recv.at[1], W),
        remote(qs, qr, rest_send.at[2], rest_recv.at[2], Z),
    ]
    for copy in low_copies + wall_copies(0, 0):
        copy.start()

    mine = jnp.broadcast_to(blocks[...].astype(F32), (CX, CX))
    theirs = jnp.broadcast_to(rows[...].astype(F32), (CX, CX))
    mine_t, theirs_t = mine.T, theirs.T
    at_row = lax.broadcasted_iota(jnp.int32, (CX, CX), 0)
    at_col = lax.broadcasted_iota(jnp.int32, (CX, CX), 1)
    alike = mine_t == mine
    rank = jnp.sum(jnp.where(alike & (at_row < at_col), 1.0, 0.0), axis=0, keepdims=True)
    code = (chunk * mine[0:1] + rank).astype(jnp.int32)
    choose_send[...] = jnp.where(
        lax.broadcasted_iota(jnp.int32, (2 * CX, CX), 0) == code, 1.0, 0.0
    ).astype(jnp.bfloat16)
    rank_t = jnp.sum(jnp.where(alike & (theirs < theirs_t), 1.0, 0.0), axis=1, keepdims=True)
    code_t = (chunk * mine_t[:, 0:1] + rank_t).astype(jnp.int32)
    choose_recv[...] = jnp.where(
        lax.broadcasted_iota(jnp.int32, (CX, 2 * CX), 1) == code_t, 1.0, 0.0
    ).astype(jnp.bfloat16)

    for copy in mid_copies + rest_copies:
        copy.start()
    for copy in low_copies:
        copy.wait()
    pl.semaphore_wait(known.at[0], len(line_x))
    for peer in line_y:
        pl.semaphore_signal(known.at[1], inc=1, device_id=peer, device_id_type=MESH)

    rows_last = row8(last)

    def unpack_rows(y, carry):
        e0, e1, w0, w1 = xr[1, 0, y], xr[1, 1, y], xr[0, 0, y], xr[0, 1, y]
        t = jnp.where(near, e0, w0)
        th[0, y + 1, tile(last)] = t
        th[0, y + 1, tile(-1)] = t
        th[0, y + 1, tile(TILES)] = th[0, y + 1, tile(0)]
        k = jnp.where(near, pltpu.roll(e0, 5, 0), pltpu.roll(w0, 3, 0))
        kb[y, tile(last)] = k
        kb[y, tile(-1)] = k
        kb[y, tile(TILES)] = kb[y, tile(0)]
        vb[0, y, rows_last] = jnp.where(near, e1, w1)
        vb[1, y, rows_last] = jnp.where(near, pltpu.roll(e1, 6, 0), pltpu.roll(w1, 2, 0))
        vb[2, y, rows_last] = jnp.where(near, pltpu.roll(e1, 4, 0), pltpu.roll(w1, 4, 0))
        hb[y, rows_last] = jnp.where(near, pltpu.roll(e1, 2, 0), pltpu.roll(w1, 6, 0))
        return carry

    def put_strip(ref, at, own_q, other_q):
        ref[0, at] = jnp.where(low_half, other_q, own_q)
        ref[1, at] = jnp.where(low_half, own_q, other_q)

    def put_static(at, at_pad, own_q, other_q):
        put_strip(sk, at_pad, own_q[0], other_q[0])
        for slot in range(2):
            t = other_q[1 + slot]
            put_strip(sv.at[2 * slot], at, own_q[1 + 2 * slot], t)
            put_strip(sv.at[2 * slot + 1], at, own_q[2 + 2 * slot], pltpu.roll(t, LZ - 4, 1))

    def split(half, value, before):
        parts = [pltpu.roll(value, (32 * (half - slot)) % LZ, 1) if slot != half else value for slot in range(4)]
        return [jnp.where(group < LOW, x, y) for x, y in zip(before, parts)] if half else parts

    def split_strips(half):
        def one(i, carry):
            at = pl.ds(pl.multiple_of(8 * i, 8), 8)
            before = [qx[0, slot, at] for slot in range(4)] if half else None
            for slot, value in enumerate(split(half, qar[half, at], before)):
                qx[half, slot, at] = value
            return carry

        lax.fori_loop(0, TILES - 1, one, 0, unroll=4)
        for side in range(2):
            before = [cx[0, side, slot] for slot in range(4)] if half else None
            for slot, value in enumerate(split(half, ca[half, side], before)):
                cx[half, side, slot] = value

    def join_rest(value, before):
        return [
            jnp.where(group < 8, x, pltpu.roll(value[slot // 2], 64, 1) if slot % 2 == 0 else value[slot // 2])
            for slot, x in enumerate(before)
        ]

    def join_strips():
        def one(i, carry):
            at = pl.ds(pl.multiple_of(8 * i, 8), 8)
            all_planes = join_rest([qr[slot, at] for slot in range(2)], [qx[1, slot, at] for slot in range(4)])
            for slot, value in enumerate(all_planes):
                qx[2, slot, at] = value
            return carry

        lax.fori_loop(0, TILES - 1, one, 0, unroll=4)
        for side in range(2):
            all_planes = join_rest([cr[side, slot] for slot in range(2)], [cx[1, side, slot] for slot in range(4)])
            for slot, value in enumerate(all_planes):
                cx[2, side, slot] = value

    def static_strips(late):
        def one(i, carry):
            at = pl.ds(pl.multiple_of(8 * i, 8), 8)
            at_pad = pl.ds(pl.multiple_of(8 * i + 8, 8), 8)
            put_strip(st.at[0], at_pad, qo[5, at], qx[late, 0, at])
            put_static(at, at_pad, [qo[slot, at] for slot in range(5)], [qx[late, slot, at] for slot in range(1, 4)])
            return carry

        lax.fori_loop(0, TILES - 1, one, 0, unroll=4)
        other = [jnp.where(near, cx[late, 1, slot], cx[late, 0, slot]) for slot in range(4)]
        put_strip(st.at[0], tile(last), edges(lambda y: th[0, y + 1, tile(last)]), other[0])
        put_static(rows_last, tile(last), pack_static(rows_last, tile(last)), other[1:])
        wrap(st.at[0])
        wrap(sk)

    def wrap(ref):
        for side in range(2):
            ref[side, tile(-1)] = ref[side, tile(last)]
            ref[side, tile(TILES)] = ref[side, tile(0)]

    def coefficients(k, k_w, k_e, k_s, k_n, k_b, k_a, v, mask_w, mask_e, bottom, top):
        v = [fluid * x for x in v]
        a_w = mask_w(0.5 * (k + k_w) + jnp.maximum(v[0], 0.0))
        a_e = mask_e(0.5 * (k + k_e) - jnp.minimum(v[0], 0.0))
        a_b = 0.5 * (k + k_b) + jnp.maximum(v[1], 0.0)
        a_b = a_b * (1.0 - metal * bottom)
        a_a = (0.5 * (k + k_a) - jnp.minimum(v[1], 0.0)) * (1.0 - top)
        a_s = 0.5 * (k + k_s) + jnp.maximum(v[2], 0.0)
        a_n = 0.5 * (k + k_n) - jnp.minimum(v[2], 0.0)
        a_d = 1.0 - (a_w + a_e + a_s + a_n + a_b + a_a)
        return a_w, a_e, a_s, a_n, a_b + metal * bottom, a_a, a_d

    whole, whole_w, whole_e = pl.ds(8, ROWS), pl.ds(7, ROWS), pl.ds(9, ROWS)
    strip_row = lax.broadcasted_iota(jnp.int32, (ROWS, LZ), 0)
    strip_group = lax.broadcasted_iota(jnp.int32, (ROWS, LZ), 1) // 8
    strip_first = strip_group == 0

    def strip_coefficients(side, carry):
        k = sk[side, whole]
        a = coefficients(
            k, sk[side, whole_w], sk[side, whole_e], pltpu.roll(k, 1, 1), pltpu.roll(k, LZ - 1, 1),
            jnp.where(strip_first, k, pltpu.roll(k, 8, 1)), pltpu.roll(k, LZ - 8, 1), [sv[d, side] for d in range(3)],
            lambda x: jnp.where(strip_row == 0, same_west * x, x),
            lambda x: jnp.where(strip_row == CX - 1, same_east * x, x),
            strip_first.astype(F32), (strip_group == CY - 1).astype(F32),
        )
        for slot, value in enumerate(a):
            sco[slot, side] = value
        return carry

    def plane_coefficients(y, carry):
        bottom = (y == 0).astype(F32)
        top = (y == CY - 1).astype(F32)
        below, above = jnp.maximum(y - 1, 0), jnp.minimum(y + 1, CY - 1)
        for i in range(TILES):
            k = kb[y, tile(i)]
            k_s, k_n = pltpu.roll(k, 1, 1), pltpu.roll(k, LZ - 1, 1)
            mask_w = (lambda x: jnp.where(sub == 0, same_west * x, x)) if i == 0 else (lambda x: x)
            mask_e = (lambda x: jnp.where(sub == 7, same_east * x, x)) if i == last - 1 else (lambda x: x)
            a = coefficients(
                k, kb[y, tile(i, -1)], kb[y, tile(i, 1)], k_s, k_n, kb[below, tile(i)], kb[above, tile(i)],
                [vb[d, y, row8(i)] for d in range(3)], mask_w, mask_e, bottom, top,
            )
            for slot, value in enumerate(a):
                co[slot, y, row8(i)] = value
        return carry

    edge_two, edge_one = (lane < 2) | (lane >= LZ - 2), first_lane | last_lane

    def sweep(t, following, step, first, end):
        def pair(g, carry):
            for half in range(2):
                y = 2 * g + half
                for i in range(TILES):
                    at = row8(i)
                    c = th[t, y + 1, tile(i)]
                    new = (
                        (hb[y, at] + co[AD, y, at] * c)
                        + (co[AW, y, at] * th[t, y + 1, tile(i, -1)] + co[AE, y, at] * th[t, y + 1, tile(i, 1)])
                        + (co[AS, y, at] * pltpu.roll(c, 1, 1) + co[AN, y, at] * pltpu.roll(c, LZ - 1, 1))
                        + (co[AB, y, at] * th[t, y, tile(i)] + co[AA, y, at] * th[t, y + 2, tile(i)])
                    )
                    if step > 0:
                        new = jnp.where(edge_two if step == 1 else edge_one, pz[step - 1, y, at], new)
                    th[following, y + 1, tile(i)] = new
                    if i == last:
                        th[following, y + 1, tile(-1)] = new
                    if i == 0:
                        th[following, y + 1, tile(TILES)] = new
            return carry

        lax.fori_loop(first, end, pair, 0)

    def strip_sweep(m, carry):
        step, side = m // 2, m % 2
        c = st[step, side, whole]
        below = jnp.where(strip_first, sw[side], pltpu.roll(c, 8, 1))
        new = (
            (sv[3, side] + sco[AD, side] * c)
            + (sco[AW, side] * st[step, side, whole_w] + sco[AE, side] * st[step, side, whole_e])
            + (sco[AS, side] * pltpu.roll(c, 1, 1) + sco[AN, side] * pltpu.roll(c, LZ - 1, 1))
            + (sco[AB, side] * below + sco[AA, side] * pltpu.roll(c, LZ - 8, 1))
        )
        st[step + 1, side, whole] = new
        st[step + 1, side, tile(-1)] = new[ROWS - 8 :]
        st[step + 1, side, tile(TILES)] = new[:8]
        return carry

    def spread(slot, first, end):
        strips = [jnp.where(low_half, st[slot + 2, 1, tile(i)], st[slot + 2, 0, tile(i)]) for i in range(TILES)]
        for y in range(first, end):
            for i in range(TILES):
                pz[slot, y, row8(i)] = pltpu.roll(strips[i], 124 - 8 * y, 1)

    def send_faces(r, t):
        field, wall = th[t, 1, own], th[t, 0, own]
        sent = fluid * (kb[0, own] * (field - wall)) + metal * field
        sb[...] = pick(choose_send[...], sent).reshape(n, chunk, LZ)

        def to(zd, i):
            x, y, c = (b // 4) % 4 + 3 - i // 4, (b // 2) % 2 + 1 - (i // 2) % 2, b % 2 + 1 - i % 2
            z = lax.rem(b // 16 + zd, n // 16)
            t = z * 16 + lax.rem(x, 4) * 4 + lax.rem(y, 2) * 2 + lax.rem(c, 2)
            remote(sb.at[t], rb.at[r, b], many_send.at[r], many_recv.at[r], (t, s)).start()

        for zd in (4, 3, 5, 2, 6, 1, 7):
            if zd < n // 16:
                lax.fori_loop(0, 16, lambda i, carry, zd=zd: (to(zd, i), carry)[1], 0, unroll=2)
        lax.fori_loop(0, 15, lambda i, carry: (to(0, i), carry)[1], 0, unroll=3)

    def receive_faces(r):
        others = pl.ds(0, n - 1)
        remote(sb.at[others], rb.at[r, others], many_send.at[r], many_recv.at[r], Z).wait()
        return pick(choose_recv[...], rb[r].reshape(2 * CX, LZ))

    def wall_strip(r):
        wall_last = jnp.where(near, wx[r, 1], wx[r, 0])
        th[3 * r, 0, tile(last)] = wall_last
        wall = th[3 * r, 0, whole]
        for t in range(4):
            if t != 3 * r:
                th[t, 0, whole] = wall
        q = qwr[r]
        for i in range(TILES - 1):
            other = pltpu.roll(q, LZ - 8 * i, 1) if i else q
            put_strip(sw, row8(i), pltpu.roll(wall[8 * i : 8 * i + 8], 4, 1), other)
        put_strip(
            sw, rows_last, pltpu.roll(wall_last, 4, 1), pltpu.roll(jnp.where(near, wc[r, 1], wc[r, 0]), 4, 1)
        )

    def theta_strips(late):
        def one(i, carry):
            at = pl.ds(pl.multiple_of(8 * i, 8), 8)
            put_strip(st.at[0], pl.ds(pl.multiple_of(8 * i + 8, 8), 8), qt[late, at], qtr[late, at])
            return carry

        lax.fori_loop(0, TILES - 1, one, 0, unroll=4)
        put_strip(
            st.at[0], tile(last), edges(lambda y: th[3, y + 1, tile(last)]), jnp.where(near, ct[late, 1], ct[late, 0])
        )
        wrap(st.at[0])

    def unpack_theta(y, carry):
        t = jnp.where(near, tr[1, y], tr[0, y])
        th[3, y + 1, tile(last)] = t
        th[3, y + 1, tile(-1)] = t
        return carry

    def send_theta(late):
        def pack(i, carry):
            at_pad = pl.ds(pl.multiple_of(8 * i + 8, 8), 8)
            at = pl.ds(pl.multiple_of(8 * i, 8), 8)
            qt[late, at] = edges(lambda y: th[3, y + 1, at_pad], CY if late else LOW)
            return carry

        lax.fori_loop(0, TILES - 1, pack, 0, unroll=4)
        for copy in theta_copies(late):
            copy.start()

    store = pltpu.make_async_copy(th.at[2, planes, own], theta_out.at[0], load_sem.at[0])

    def by(p, *values):
        out = values[0] + p * (values[1] - values[0])
        if len(values) == 3:
            out = out + p * (p - 1) // 2 * (values[2] - 2 * values[1] + values[0])
        return out

    def sweeps(r, p, *bounds):
        for step in range(SWEEPS):
            first, end = zip(*[bound[step] for bound in bounds])
            sweep((3 * r + step) % 4, (3 * r + step + 1) % 4, step, by(p, *first), by(p, *end))

    def when(p, value, action):
        pl.when(p == value)(action)

    def unpack(take, first, end):
        lax.fori_loop(first, end, take, 0, unroll=4)

    def spread_both(first, end):
        for slot in range(2):
            spread(slot, first, end)

    for copy in wall_copies(0, 0):
        copy.wait()
    wall_strip(0)

    def first_iteration(p, carry):
        @pl.when(p == 0)
        def _():
            split_strips(0)
            unpack(unpack_rows, 0, LOW)

        @pl.when(p == 1)
        def _():
            for copy in mid_copies:
                copy.wait()
            split_strips(1)
            unpack(unpack_rows, LOW, 2 * LOW)

        @pl.when(p == 2)
        def _():
            for copy in rest_copies:
                copy.wait()
            join_strips()
            unpack(unpack_rows, 2 * LOW, CY)

        static_strips(p)
        lax.fori_loop(0, 2, strip_coefficients, 0)
        lax.fori_loop(0, 2 * SWEEPS, strip_sweep, 0)
        when(p, 0, lambda: spread_both(0, 4))
        when(p, 1, lambda: spread_both(0, 8))
        when(p, 2, lambda: spread_both(4, CY))
        lax.fori_loop(by(p, 0, 3, 7), by(p, 4, 8, CY), plane_coefficients, 0)
        sweeps(0, p, ((0, 2), (0, 1), (0, 1)), ((1, 4), (1, 3), (0, 2)), ((3, 8), (3, 8), (2, 8)))

        @pl.when(p == 0)
        def _():
            pl.semaphore_wait(known.at[1], len(line_y))
            send_faces(0, 3)

        @pl.when(p == 1)
        def _():
            send_theta(0)
            th[3, 0, own] = receive_faces(0)
            pack_wall(1, 3)
            for copy in wall_copies(1, 3):
                copy.start()

        return carry

    lax.fori_loop(0, 3, first_iteration, 0)

    send_theta(1)
    for copy in theta_copies(0):
        copy.wait()
    unpack(unpack_theta, 0, LOW)
    for copy in wall_copies(1, 3):
        copy.wait()
    wall_strip(1)

    def second_iteration(p, carry):
        @pl.when(p == 1)
        def _():
            for copy in theta_copies(1):
                copy.wait()
            unpack(unpack_theta, LOW, CY)

        theta_strips(p)
        lax.fori_loop(0, 2 * SWEEPS, strip_sweep, 0)
        when(p, 0, lambda: spread_both(0, 4))
        when(p, 1, lambda: spread_both(0, CY))
        sweeps(1, p, ((0, 2), (0, 1), (0, 1)), ((1, 8), (1, 8), (0, 8)))

        @pl.when(p == 0)
        def _():
            send_faces(1, 2)

        return carry

    lax.fori_loop(0, 2, second_iteration, 0)
    store.start()
    th[2, 0, own] = receive_faces(1)
    wall_out[0] = th[2, 0, own]
    store.wait()


def publish(theta, wall, theta_out, wall_out, field, rows, come, go):
    half = pl.ds(0, CY // 2), pl.ds(CY // 2, CY // 2)
    parts = [(theta.at[0, at], field.at[at], theta_out.at[0, at]) for at in half]
    parts.append((wall.at[0], rows, wall_out.at[0]))
    take = [pltpu.make_async_copy(source, here, come.at[i]) for i, (source, here, _) in enumerate(parts)]
    give = [pltpu.make_async_copy(here, target, go.at[i]) for i, (_, here, target) in enumerate(parts)]
    for copy in take:
        copy.start()
    for first, second in zip(take, give):
        first.wait()
        second.start()
    for copy in give:
        copy.wait()


def solution(mesh):
    n = mesh.shape["blk"]
    chunk = 2 * CX // n

    def part(theta, cond, vel, heat, wall, kinds, blocks, rows):
        hbm = pl.BlockSpec(memory_space=pltpu.HBM)
        anywhere = pl.BlockSpec(memory_space=pl.ANY)
        vmem = pl.BlockSpec(memory_space=pltpu.VMEM)
        buf = lambda *shape: pltpu.VMEM(shape, F32)
        held = pl.pallas_call(
            functools.partial(kernel, n),
            out_shape=(
                jax.ShapeDtypeStruct(theta.shape, F32),
                jax.ShapeDtypeStruct(wall.shape, F32),
            ),
            in_specs=[hbm] * 8,
            out_specs=(anywhere, vmem),
            scratch_shapes=[
                buf(4, CY + 2, PAD, LZ),
                buf(CY, PAD, LZ),
                buf(3, CY, ROWS, LZ),
                buf(CY, ROWS, LZ),
                buf(7, CY, ROWS, LZ),
                buf(4, 2, PAD, LZ),
                buf(2, PAD, LZ),
                buf(4, 2, ROWS, LZ),
                buf(7, 2, ROWS, LZ),
                buf(2, ROWS, LZ),
                buf(2, CY, ROWS, LZ),
                buf(2, 2, CY, 8, LZ),
                buf(2, 2, CY, 8, LZ),
                buf(6, CX, LZ),
                buf(2, CX, LZ),
                buf(2, CX, LZ),
                buf(2, 2, 8, LZ),
                buf(3, 4, CX, LZ),
                buf(3, 2, 4, 8, LZ),
                buf(2, CX, LZ),
                buf(2, CX, LZ),
                buf(2, 2, 8, LZ),
                buf(2, CX, LZ),
                buf(2, CX, LZ),
                buf(2, 2, 8, LZ),
                buf(2, 8, LZ),
                buf(2, 8, LZ),
                buf(2, 2, 8, LZ),
                buf(2, 2, 8, LZ),
                buf(2, CY, 8, LZ),
                buf(n, chunk, LZ),
                buf(2, n, chunk, LZ),
                pltpu.VMEM((2 * CX, CX), jnp.bfloat16),
                pltpu.VMEM((CX, 2 * CX), jnp.bfloat16),
                pltpu.SMEM((n,), jnp.int32),
                pltpu.VMEM((1, CX), jnp.int32),
                pltpu.VMEM((1, CX), jnp.int32),
                pltpu.SemaphoreType.DMA((8,)),
                pltpu.SemaphoreType.DMA((5,)),
                pltpu.SemaphoreType.DMA((5,)),
                pltpu.SemaphoreType.DMA((5,)),
                pltpu.SemaphoreType.DMA((5,)),
                pltpu.SemaphoreType.DMA((5,)),
                pltpu.SemaphoreType.DMA((5,)),
                pltpu.SemaphoreType.DMA((2, 5)),
                pltpu.SemaphoreType.DMA((2, 5)),
                pltpu.SemaphoreType.DMA((2, 5)),
                pltpu.SemaphoreType.DMA((2, 5)),
                pltpu.SemaphoreType.DMA((2,)),
                pltpu.SemaphoreType.DMA((2,)),
                pltpu.SemaphoreType.REGULAR((2,)),
            ],
            compiler_params=pltpu.CompilerParams(
                collective_id=0, has_side_effects=True, vmem_limit_bytes=56 * 2**20
            ),
        )(theta, cond, vel, heat, wall, kinds, blocks, rows)
        return pl.pallas_call(
            publish,
            out_shape=tuple(jax.ShapeDtypeStruct(x.shape, F32) for x in held),
            in_specs=[anywhere] * 2,
            out_specs=(anywhere, anywhere),
            scratch_shapes=[
                buf(CY, CX, LZ),
                buf(CX, LZ),
                pltpu.SemaphoreType.DMA((3,)),
                pltpu.SemaphoreType.DMA((3,)),
            ],
        )(*held)

    whole = P("blk", None, None, "span")
    rows = P("blk", None, "span")
    return jax.shard_map(
        part,
        mesh=mesh,
        in_specs=(whole, whole, P("blk", None, None, None, "span"), whole, rows, P(), P("blk", None), P("blk", None)),
        out_specs=(whole, rows),
        check_vma=False,
    )
```

```python
import functools

import jax
import jax.numpy as jnp
from jax import lax
from jax.experimental import pallas as pl
from jax.experimental.pallas import tpu as pltpu
from jax.sharding import PartitionSpec as P

MESH = pl.DeviceIdType.MESH
ITERS, SWEEPS = 2, 3
CY, CX, LZ = 16, 128, 128
LOW = 4
TILES = CX // 8 + 1
ROWS = 8 * TILES
PAD = ROWS + 16
F32 = jnp.float32
AW, AE, AS, AN, AB, AA, AD, SRC = range(8)


def tile(i, shift=0):
    return pl.ds(8 + 8 * i + shift, 8)


def row8(i):
    return pl.ds(8 * i, 8)


def remote(src, dst, send, recv, device):
    return pltpu.make_async_remote_copy(
        src_ref=src, dst_ref=dst, send_sem=send, recv_sem=recv, device_id=device, device_id_type=MESH
    )


def split3(x):
    hi = x.astype(jnp.bfloat16)
    rest = x - hi.astype(F32)
    mid = rest.astype(jnp.bfloat16)
    low = (rest - mid.astype(F32)).astype(jnp.bfloat16)
    return hi, mid, low


def pick(chooser, x):
    return sum(jnp.dot(chooser, part, preferred_element_type=F32) for part in split3(x))


def kernel(
    n, theta_ref, cond_ref, vel_ref, heat_ref, wall_ref, kind_ref, block_ref, row_ref,
    theta_out, wall_out,
    th, kb, vb, hb, co, st, sk, sv, sco, sw, pz,
    xs, xr, qo, hq, qs, qr, cr, qx, cx, qa, qar, ca, qt, qtr, ct, qw, qwr, wx, wc, tr,
    sb, rb, choose_send, choose_recv, kinds, blocks, rows,
    load_sem, low_send, low_recv, rest_send, rest_recv, wall_send, wall_recv, theta_send, theta_recv,
    many_send, many_recv, known,
):
    b, s = lax.axis_index("blk"), lax.axis_index("span")
    chunk = 2 * CX // n
    east, west = lax.rem(b + 1, n), lax.rem(b + n - 1, n)
    E, W, Z, ZE, ZW = (east, s), (west, s), (b, 1 - s), (east, 1 - s), (west, 1 - s)
    own, planes = pl.ds(8, CX), pl.ds(1, CY)

    def line(count, stride):
        at = lax.rem(b // stride, count)
        return [(b + (lax.rem(at + d, count) - at) * stride, s) for d in range(1, count)]

    line_z, line_x, line_y = line(n // 16, 16), line(4, 4), line(4, 1)
    barrier = pltpu.get_barrier_semaphore()
    beside = [E, W, Z, ZE, ZW] + line_z + line_x + line_y
    for peer in beside:
        pl.semaphore_signal(barrier, inc=1, device_id=peer, device_id_type=MESH)

    loads = [
        pltpu.make_async_copy(kind_ref, kinds, load_sem.at[5]),
        pltpu.make_async_copy(block_ref, blocks, load_sem.at[6]),
        pltpu.make_async_copy(row_ref, rows, load_sem.at[7]),
        pltpu.make_async_copy(theta_ref.at[0], th.at[0, planes, own], load_sem.at[0]),
        pltpu.make_async_copy(cond_ref.at[0], kb.at[:, own], load_sem.at[1]),
        pltpu.make_async_copy(vel_ref.at[0], vb.at[:, :, pl.ds(0, CX)], load_sem.at[2]),
        pltpu.make_async_copy(heat_ref.at[0], hb.at[:, pl.ds(0, CX)], load_sem.at[3]),
        pltpu.make_async_copy(wall_ref.at[0], th.at[0, 0, own], load_sem.at[4]),
    ]
    for load in loads:
        load.start()

    rb[:, pl.ds(b, 1)] = jnp.zeros((2, 1, chunk, LZ), F32)

    lane = lax.broadcasted_iota(jnp.int32, (8, LZ), 1)
    sub = lax.broadcasted_iota(jnp.int32, (8, LZ), 0)
    group, place = lane // 8, lane % 8
    first_lane, last_lane = lane == 0, lane == LZ - 1
    low_half = place < 4
    middle = (place >= 2) & (place < 6)
    near = sub < 4
    last = TILES - 1

    for t in range(4):
        th[t, CY + 1] = jnp.zeros((PAD, LZ), F32)

    for load in loads:
        load.wait()
    fluid = kinds[b].astype(F32)
    metal = 1.0 - fluid
    same_west = 1.0 - jnp.abs(kinds[west].astype(F32) - fluid)
    same_east = 1.0 - jnp.abs(kinds[east].astype(F32) - fluid)

    def edges(load, count=CY):
        out = pltpu.roll(load(0), 4, 1)
        for y in range(1, count):
            out = jnp.where(group == y, pltpu.roll(load(y), (8 * y + 4) % LZ, 1), out)
        return out

    def pack_static(at, at_pad, count=CY):
        q_k = edges(lambda y: kb[y, at_pad], count)
        q_v = [edges(lambda y, d=d: vb[d, y, at], count) for d in range(3)]
        q_h = edges(lambda y: hb[y, at], count)
        return [q_k] + q_v + [q_h]

    def beside_middle(x):
        return jnp.where(place >= 6, pltpu.roll(x, 4, 1), pltpu.roll(x, LZ - 4, 1))

    def from_beside(x):
        return jnp.where(low_half, pltpu.roll(x, LZ - 4, 1), pltpu.roll(x, 4, 1))

    def paired(q):
        return [
            q[0],
            jnp.where(middle, q[1], beside_middle(q[2])),
            jnp.where(middle, q[3], beside_middle(q[4])),
        ]

    def pack_low(i, carry):
        at = pl.ds(pl.multiple_of(8 * i, 8), 8)
        at_pad = pl.ds(pl.multiple_of(8 * i + 8, 8), 8)
        q = pack_static(at, at_pad, LOW) + [edges(lambda y: th[0, y + 1, at_pad], LOW)]
        sent = [q[5]] + paired(q)
        out = sent[0]
        for slot in range(1, 4):
            out = jnp.where(group >= LOW * slot, pltpu.roll(sent[slot], 8 * LOW * slot, 1), out)
        qa[at] = out
        return carry

    def pack_tile(i, carry):
        at = pl.ds(pl.multiple_of(8 * i, 8), 8)
        at_pad = pl.ds(pl.multiple_of(8 * i + 8, 8), 8)
        q = pack_static(at, at_pad) + [edges(lambda y: th[0, y + 1, at_pad])]
        sent = [q[5]] + paired(q)
        rest = [jnp.where(group < LOW, pltpu.roll(sent[3], LZ - 32 * (m + 1), 1), sent[m]) for m in range(3)]
        for slot in range(6):
            qo[slot, at] = q[slot]
        for slot in range(3):
            qs[slot, at] = rest[slot]
        return carry

    lax.fori_loop(0, TILES - 1, pack_low, 0, unroll=4)

    def pack_rows(y, carry):
        end, pad_end = pl.ds(CX - 8, 8), pl.ds(CX, 8)
        xs[0, 0, y] = jnp.where(sub >= 5, th[0, y + 1, pad_end], pltpu.roll(kb[y, pad_end], 5, 0))
        xs[0, 1, y] = jnp.where(
            sub >= 6,
            vb[0, y, end],
            jnp.where(
                sub >= 4,
                pltpu.roll(vb[1, y, end], 6, 0),
                jnp.where(sub >= 2, pltpu.roll(vb[2, y, end], 4, 0), pltpu.roll(hb[y, end], 2, 0)),
            ),
        )
        zero, pad_zero = pl.ds(0, 8), pl.ds(8, 8)
        xs[1, 0, y] = jnp.where(sub < 3, th[0, y + 1, pad_zero], pltpu.roll(kb[y, pad_zero], 3, 0))
        xs[1, 1, y] = jnp.where(
            sub < 2,
            vb[0, y, zero],
            jnp.where(
                sub < 4,
                pltpu.roll(vb[1, y, zero], 2, 0),
                jnp.where(sub < 6, pltpu.roll(vb[2, y, zero], 4, 0), pltpu.roll(hb[y, zero], 6, 0)),
            ),
        )
        return carry

    lax.fori_loop(0, CY, pack_rows, 0, unroll=4)

    def pack_wall(r, t):
        out = pltpu.roll(th[t, 0, tile(0)], 4, 1)
        for i in range(1, TILES - 1):
            out = jnp.where(group == i, pltpu.roll(th[t, 0, tile(i)], (8 * i + 4) % LZ, 1), out)
        qw[r] = out

    pack_wall(0, 0)

    pl.semaphore_wait(barrier, len(beside))
    for peer in line_x:
        pl.semaphore_signal(known.at[0], inc=1, device_id=peer, device_id_type=MESH)

    def wall_copies(r, t):
        plane, ss, rs = th.at[t, 0], wall_send.at[r], wall_recv.at[r]
        tail, head = plane.at[pl.ds(CX, 8)], plane.at[pl.ds(8, 8)]
        return [
            remote(tail, wc.at[r, 0], ss.at[3], rs.at[3], ZE),
            remote(head, wc.at[r, 1], ss.at[4], rs.at[4], ZW),
            remote(tail, wx.at[r, 0], ss.at[0], rs.at[0], E),
            remote(head, wx.at[r, 1], ss.at[1], rs.at[1], W),
            remote(qw.at[r], qwr.at[r], ss.at[2], rs.at[2], Z),
        ]

    head, tail = pl.ds(0, 8), pl.ds(CX - 8, 8)
    low, rest = pl.ds(0, LOW), pl.ds(LOW, CY - LOW)

    def theta_copies(late):
        ss, rs = theta_send.at[late], theta_recv.at[late]
        at, to = (pl.ds(1 + LOW, CY - LOW), pl.ds(LOW, CY - LOW)) if late else (pl.ds(1, LOW), low)
        return [
            remote(qt.at[late, tail], ct.at[late, 0], ss.at[1], rs.at[1], ZE),
            remote(qt.at[late, head], ct.at[late, 1], ss.at[2], rs.at[2], ZW),
            remote(th.at[3, at, pl.ds(CX, 8)], tr.at[0, to], ss.at[3], rs.at[3], E),
            remote(th.at[3, at, pl.ds(8, 8)], tr.at[1, to], ss.at[4], rs.at[4], W),
            remote(qt.at[late], qtr.at[late], ss.at[0], rs.at[0], Z),
        ]

    low_copies = [
        remote(qa.at[tail], ca.at[0], low_send.at[3], low_recv.at[3], ZE),
        remote(qa.at[head], ca.at[1], low_send.at[4], low_recv.at[4], ZW),
        remote(xs.at[0, :, low], xr.at[0, :, low], low_send.at[0], low_recv.at[0], E),
        remote(xs.at[1, :, low], xr.at[1, :, low], low_send.at[1], low_recv.at[1], W),
        remote(qa, qar, low_send.at[2], low_recv.at[2], Z),
    ]
    rest_copies = [
        remote(qs.at[:, tail], cr.at[0], rest_send.at[3], rest_recv.at[3], ZE),
        remote(qs.at[:, head], cr.at[1], rest_send.at[4], rest_recv.at[4], ZW),
        remote(xs.at[0, :, rest], xr.at[0, :, rest], rest_send.at[0], rest_recv.at[0], E),
        remote(xs.at[1, :, rest], xr.at[1, :, rest], rest_send.at[1], rest_recv.at[1], W),
        remote(qs, qr, rest_send.at[2], rest_recv.at[2], Z),
    ]
    for copy in low_copies + wall_copies(0, 0):
        copy.start()

    lax.fori_loop(0, TILES - 1, pack_tile, 0, unroll=2)
    for copy in rest_copies:
        copy.start()

    mine = jnp.broadcast_to(blocks[...].astype(F32), (CX, CX))
    theirs = jnp.broadcast_to(rows[...].astype(F32), (CX, CX))
    mine_t, theirs_t = mine.T, theirs.T
    at_row = lax.broadcasted_iota(jnp.int32, (CX, CX), 0)
    at_col = lax.broadcasted_iota(jnp.int32, (CX, CX), 1)
    alike = mine_t == mine
    rank = jnp.sum(jnp.where(alike & (at_row < at_col), 1.0, 0.0), axis=0, keepdims=True)
    code = (chunk * mine[0:1] + rank).astype(jnp.int32)
    choose_send[...] = jnp.where(
        lax.broadcasted_iota(jnp.int32, (2 * CX, CX), 0) == code, 1.0, 0.0
    ).astype(jnp.bfloat16)
    rank_t = jnp.sum(jnp.where(alike & (theirs < theirs_t), 1.0, 0.0), axis=1, keepdims=True)
    code_t = (chunk * mine_t[:, 0:1] + rank_t).astype(jnp.int32)
    choose_recv[...] = jnp.where(
        lax.broadcasted_iota(jnp.int32, (CX, 2 * CX), 1) == code_t, 1.0, 0.0
    ).astype(jnp.bfloat16)

    rows_last = row8(last)

    def unpack_rows(y, carry):
        e0, e1, w0, w1 = xr[1, 0, y], xr[1, 1, y], xr[0, 0, y], xr[0, 1, y]
        t = jnp.where(near, e0, w0)
        th[0, y + 1, tile(last)] = t
        th[0, y + 1, tile(-1)] = t
        th[0, y + 1, tile(TILES)] = th[0, y + 1, tile(0)]
        k = jnp.where(near, pltpu.roll(e0, 5, 0), pltpu.roll(w0, 3, 0))
        kb[y, tile(last)] = k
        kb[y, tile(-1)] = k
        kb[y, tile(TILES)] = kb[y, tile(0)]
        vb[0, y, rows_last] = jnp.where(near, e1, w1)
        vb[1, y, rows_last] = jnp.where(near, pltpu.roll(e1, 6, 0), pltpu.roll(w1, 2, 0))
        vb[2, y, rows_last] = jnp.where(near, pltpu.roll(e1, 4, 0), pltpu.roll(w1, 4, 0))
        hb[y, rows_last] = jnp.where(near, pltpu.roll(e1, 2, 0), pltpu.roll(w1, 6, 0))
        return carry

    def put_strip(ref, at, own_q, other_q):
        ref[0, at] = jnp.where(low_half, other_q, own_q)
        ref[1, at] = jnp.where(low_half, own_q, other_q)

    def put_static(at, at_pad, own_q, other_q):
        put_strip(sk, at_pad, own_q[0], other_q[0])
        for slot in range(2):
            t = other_q[1 + slot]
            put_strip(sv.at[2 * slot], at, own_q[1 + 2 * slot], t)
            put_strip(sv.at[2 * slot + 1], at, own_q[2 + 2 * slot], from_beside(t))

    def split(value):
        return [pltpu.roll(value, LZ - 32 * slot, 1) if slot else value for slot in range(4)]

    def join(value, before):
        out = [jnp.where(group < LOW, x, y) for x, y in zip(before, value)]
        fourth = before[3]
        for m in range(3):
            fourth = jnp.where(group >= LOW * (m + 1), pltpu.roll(value[m], 32 * (m + 1), 1), fourth)
        return out + [fourth]

    def take_strips(late):
        def one(i, carry):
            at = pl.ds(pl.multiple_of(8 * i, 8), 8)
            if late:
                out = join([qr[m, at] for m in range(3)], [qx[0, slot, at] for slot in range(4)])
            else:
                out = split(qar[at])
            for slot, value in enumerate(out):
                qx[late, slot, at] = value
            return carry

        lax.fori_loop(0, TILES - 1, one, 0, unroll=4)
        for side in range(2):
            if late:
                out = join([cr[side, m] for m in range(3)], [cx[0, side, slot] for slot in range(4)])
            else:
                out = split(ca[side])
            for slot, value in enumerate(out):
                cx[late, side, slot] = value

    def pack_halo(count):
        q = pack_static(rows_last, tile(last), count) + [edges(lambda y: th[0, y + 1, tile(last)], count)]
        for slot in range(6):
            hq[slot] = q[slot]

    def static_strips(late):
        def one(i, carry):
            at = pl.ds(pl.multiple_of(8 * i, 8), 8)
            at_pad = pl.ds(pl.multiple_of(8 * i + 8, 8), 8)
            put_strip(st.at[0], at_pad, qo[5, at], qx[late, 0, at])
            put_static(at, at_pad, [qo[slot, at] for slot in range(5)], [qx[late, slot, at] for slot in range(1, 4)])
            return carry

        lax.fori_loop(0, TILES - 1, one, 0, unroll=4)
        other = [jnp.where(near, cx[late, 1, slot], cx[late, 0, slot]) for slot in range(4)]
        put_strip(st.at[0], tile(last), hq[5], other[0])
        put_static(rows_last, tile(last), [hq[slot] for slot in range(5)], other[1:])
        wrap(st.at[0])
        wrap(sk)

    def wrap(ref):
        for side in range(2):
            ref[side, tile(-1)] = ref[side, tile(last)]
            ref[side, tile(TILES)] = ref[side, tile(0)]

    def coefficients(k, k_w, k_e, k_s, k_n, k_b, k_a, v, mask_w, mask_e, bottom, top):
        v = [fluid * x for x in v]
        a_w = mask_w(0.5 * (k + k_w) + jnp.maximum(v[0], 0.0))
        a_e = mask_e(0.5 * (k + k_e) - jnp.minimum(v[0], 0.0))
        a_b = 0.5 * (k + k_b) + jnp.maximum(v[1], 0.0)
        a_b = a_b * (1.0 - metal * bottom)
        a_a = (0.5 * (k + k_a) - jnp.minimum(v[1], 0.0)) * (1.0 - top)
        a_s = 0.5 * (k + k_s) + jnp.maximum(v[2], 0.0)
        a_n = 0.5 * (k + k_n) - jnp.minimum(v[2], 0.0)
        a_d = 1.0 - (a_w + a_e + a_s + a_n + a_b + a_a)
        return a_w, a_e, a_s, a_n, a_b + metal * bottom, a_a, a_d

    whole, whole_w, whole_e = pl.ds(8, ROWS), pl.ds(7, ROWS), pl.ds(9, ROWS)
    strip_row = lax.broadcasted_iota(jnp.int32, (ROWS, LZ), 0)
    strip_group = lax.broadcasted_iota(jnp.int32, (ROWS, LZ), 1) // 8
    strip_first = strip_group == 0

    def strip_coefficients():
        both = []
        for side in range(2):
            k = sk[side, whole]
            both.append(coefficients(
                k, sk[side, whole_w], sk[side, whole_e], pltpu.roll(k, 1, 1), pltpu.roll(k, LZ - 1, 1),
                jnp.where(strip_first, k, pltpu.roll(k, 8, 1)), pltpu.roll(k, LZ - 8, 1),
                [sv[d, side] for d in range(3)],
                lambda x: jnp.where(strip_row == 0, same_west * x, x),
                lambda x: jnp.where(strip_row == CX - 1, same_east * x, x),
                strip_first.astype(F32), (strip_group == CY - 1).astype(F32),
            ))
        for side, a in enumerate(both):
            for slot, value in enumerate(a):
                sco[slot, side] = value

    def plane_coefficients(tiles):
        def one(y, carry):
            bottom = (y == 0).astype(F32)
            top = (y == CY - 1).astype(F32)
            below, above = jnp.maximum(y - 1, 0), jnp.minimum(y + 1, CY - 1)
            for i in tiles:
                k = kb[y, tile(i)]
                k_s, k_n = pltpu.roll(k, 1, 1), pltpu.roll(k, LZ - 1, 1)
                mask_w = (lambda x: jnp.where(sub == 0, same_west * x, x)) if i == 0 else (lambda x: x)
                mask_e = (lambda x: jnp.where(sub == 7, same_east * x, x)) if i == last - 1 else (lambda x: x)
                a = coefficients(
                    k, kb[y, tile(i, -1)], kb[y, tile(i, 1)], k_s, k_n, kb[below, tile(i)], kb[above, tile(i)],
                    [vb[d, y, row8(i)] for d in range(3)], mask_w, mask_e, bottom, top,
                )
                for slot, value in enumerate(a):
                    co[slot, y, row8(i)] = value
            return carry

        return one

    inner = plane_coefficients(range(1, last - 1))
    outer = plane_coefficients((0, last - 1, last))

    lax.fori_loop(0, CY, inner, 0, unroll=2)

    for copy in low_copies:
        copy.wait()
    pl.semaphore_wait(known.at[0], len(line_x))
    for peer in line_y:
        pl.semaphore_signal(known.at[1], inc=1, device_id=peer, device_id_type=MESH)

    edge_two, edge_one = (lane < 2) | (lane >= LZ - 2), first_lane | last_lane

    def sweep(t, following, step, first, end, size):
        def some(g, carry):
            for m in range(size):
                y = size * g + m
                for i in range(TILES):
                    at = row8(i)
                    c = th[t, y + 1, tile(i)]
                    new = (
                        (hb[y, at] + co[AD, y, at] * c)
                        + (co[AW, y, at] * th[t, y + 1, tile(i, -1)] + co[AE, y, at] * th[t, y + 1, tile(i, 1)])
                        + (co[AS, y, at] * pltpu.roll(c, 1, 1) + co[AN, y, at] * pltpu.roll(c, LZ - 1, 1))
                        + (co[AB, y, at] * th[t, y, tile(i)] + co[AA, y, at] * th[t, y + 2, tile(i)])
                    )
                    if step > 0:
                        new = jnp.where(edge_two if step == 1 else edge_one, pz[step - 1, y, at], new)
                    th[following, y + 1, tile(i)] = new
                    if i == last:
                        th[following, y + 1, tile(-1)] = new
                    if i == 0:
                        th[following, y + 1, tile(TILES)] = new
            return carry

        lax.fori_loop(first, end, some, 0)

    first_group = group == 0

    def strip_sweeps():
        for step in range(SWEEPS):
            for side in range(2):
                for i in range(TILES):
                    at = row8(i)
                    c = st[step, side, tile(i)]
                    below = jnp.where(first_group, sw[side, at], pltpu.roll(c, 8, 1))
                    new = (
                        (sv[3, side, at] + sco[AD, side, at] * c)
                        + (sco[AW, side, at] * st[step, side, tile(i, -1)] + sco[AE, side, at] * st[step, side, tile(i, 1)])
                        + (sco[AS, side, at] * pltpu.roll(c, 1, 1) + sco[AN, side, at] * pltpu.roll(c, LZ - 1, 1))
                        + (sco[AB, side, at] * below + sco[AA, side, at] * pltpu.roll(c, LZ - 8, 1))
                    )
                    st[step + 1, side, tile(i)] = new
                    if i == last:
                        st[step + 1, side, tile(-1)] = new
                    if i == 0:
                        st[step + 1, side, tile(TILES)] = new

    def spread(slot, first, end):
        strips = [jnp.where(low_half, st[slot + 2, 1, tile(i)], st[slot + 2, 0, tile(i)]) for i in range(TILES)]
        for y in range(first, end):
            for i in range(TILES):
                pz[slot, y, row8(i)] = pltpu.roll(strips[i], 124 - 8 * y, 1)

    def send_faces(r, t):
        field, wall = th[t, 1, own], th[t, 0, own]
        sent = fluid * (kb[0, own] * (field - wall)) + metal * field
        sb[...] = pick(choose_send[...], sent).reshape(n, chunk, LZ)

        def to(zd, i):
            x, y, c = (b // 4) % 4 + 3 - i // 4, (b // 2) % 2 + 1 - (i // 2) % 2, b % 2 + 1 - i % 2
            z = lax.rem(b // 16 + zd, n // 16)
            t = z * 16 + lax.rem(x, 4) * 4 + lax.rem(y, 2) * 2 + lax.rem(c, 2)
            remote(sb.at[t], rb.at[r, b], many_send.at[r], many_recv.at[r], (t, s)).start()

        for zd in (4, 3, 5, 2, 6, 1, 7):
            if zd < n // 16:
                lax.fori_loop(0, 16, lambda i, carry, zd=zd: (to(zd, i), carry)[1], 0, unroll=2)
        lax.fori_loop(0, 15, lambda i, carry: (to(0, i), carry)[1], 0, unroll=3)

    def receive_faces(r):
        others = pl.ds(0, n - 1)
        remote(sb.at[others], rb.at[r, others], many_send.at[r], many_recv.at[r], Z).wait()
        return pick(choose_recv[...], rb[r].reshape(2 * CX, LZ))

    def wall_strip(r):
        wall_last = jnp.where(near, wx[r, 1], wx[r, 0])
        th[3 * r, 0, tile(last)] = wall_last
        wall = th[3 * r, 0, whole]
        for t in range(4):
            if t != 3 * r:
                th[t, 0, whole] = wall
        q = qwr[r]
        for i in range(TILES - 1):
            other = pltpu.roll(q, LZ - 8 * i, 1) if i else q
            put_strip(sw, row8(i), pltpu.roll(wall[8 * i : 8 * i + 8], 4, 1), other)
        put_strip(
            sw, rows_last, pltpu.roll(wall_last, 4, 1), pltpu.roll(jnp.where(near, wc[r, 1], wc[r, 0]), 4, 1)
        )

    def theta_strips(late):
        def one(i, carry):
            at = pl.ds(pl.multiple_of(8 * i, 8), 8)
            put_strip(st.at[0], pl.ds(pl.multiple_of(8 * i + 8, 8), 8), qt[late, at], qtr[late, at])
            return carry

        lax.fori_loop(0, TILES - 1, one, 0, unroll=4)
        put_strip(
            st.at[0], tile(last), edges(lambda y: th[3, y + 1, tile(last)], CY if late else LOW), jnp.where(near, ct[late, 1], ct[late, 0])
        )
        wrap(st.at[0])

    def unpack_theta(y, carry):
        t = jnp.where(near, tr[1, y], tr[0, y])
        th[3, y + 1, tile(last)] = t
        th[3, y + 1, tile(-1)] = t
        return carry

    def send_theta(late):
        def pack(i, carry):
            at_pad = pl.ds(pl.multiple_of(8 * i + 8, 8), 8)
            at = pl.ds(pl.multiple_of(8 * i, 8), 8)
            qt[late, at] = edges(lambda y: th[3, y + 1, at_pad], CY if late else LOW)
            return carry

        lax.fori_loop(0, TILES - 1, pack, 0, unroll=4)
        for copy in theta_copies(late):
            copy.start()

    store = pltpu.make_async_copy(th.at[2, planes, own], theta_out.at[0], load_sem.at[0])

    def early_sweeps(r):
        for step, pairs in enumerate((2, 1, 1)):
            sweep((3 * r + step) % 4, (3 * r + step + 1) % 4, step, 0, pairs, 2)

    def late_sweeps(r):
        for step in range(SWEEPS):
            sweep((3 * r + step) % 4, (3 * r + step + 1) % 4, step, 0, CY // 4, 4)

    def when(p, value, action):
        pl.when(p == value)(action)

    def unpack(take, first, end):
        lax.fori_loop(first, end, take, 0, unroll=4)

    def spread_both(first, end):
        for slot in range(2):
            spread(slot, first, end)

    for copy in wall_copies(0, 0):
        copy.wait()
    wall_strip(0)

    def first_iteration(p, carry):
        @pl.when(p == 0)
        def _():
            take_strips(0)
            unpack(unpack_rows, 0, LOW)
            pack_halo(LOW)
            lax.fori_loop(0, LOW, outer, 0, unroll=4)

        @pl.when(p == 1)
        def _():
            for copy in rest_copies:
                copy.wait()
            take_strips(1)
            unpack(unpack_rows, LOW, CY)
            pack_halo(CY)
            lax.fori_loop(0, CY, outer, 0, unroll=4)

        static_strips(p)
        strip_coefficients()
        strip_sweeps()
        when(p, 0, lambda: spread_both(0, 4))
        when(p, 1, lambda: spread_both(0, CY))
        when(p, 0, lambda: early_sweeps(0))
        when(p, 1, lambda: late_sweeps(0))

        @pl.when(p == 0)
        def _():
            pl.semaphore_wait(known.at[1], len(line_y))
            send_faces(0, 3)

        return carry

    lax.fori_loop(0, 2, first_iteration, 0)

    send_theta(0)
    th[3, 0, own] = receive_faces(0)
    pack_wall(1, 3)
    for copy in wall_copies(1, 3):
        copy.start()
    send_theta(1)
    for copy in theta_copies(0):
        copy.wait()
    unpack(unpack_theta, 0, LOW)
    theta_strips(0)
    for copy in wall_copies(1, 3):
        copy.wait()
    wall_strip(1)

    def second_iteration(p, carry):
        @pl.when(p == 1)
        def _():
            for copy in theta_copies(1):
                copy.wait()
            unpack(unpack_theta, LOW, CY)
            theta_strips(1)

        strip_sweeps()
        when(p, 0, lambda: spread_both(0, 4))
        when(p, 1, lambda: spread_both(0, CY))
        when(p, 0, lambda: early_sweeps(1))
        when(p, 1, lambda: late_sweeps(1))

        @pl.when(p == 0)
        def _():
            send_faces(1, 2)

        return carry

    lax.fori_loop(0, 2, second_iteration, 0)
    store.start()
    th[2, 0, own] = receive_faces(1)
    wall_out[0] = th[2, 0, own]
    store.wait()


def publish(theta, wall, theta_out, wall_out, field, rows, come, go):
    half = pl.ds(0, CY // 2), pl.ds(CY // 2, CY // 2)
    parts = [(theta.at[0, at], field.at[at], theta_out.at[0, at]) for at in half]
    parts.append((wall.at[0], rows, wall_out.at[0]))
    take = [pltpu.make_async_copy(source, here, come.at[i]) for i, (source, here, _) in enumerate(parts)]
    give = [pltpu.make_async_copy(here, target, go.at[i]) for i, (_, here, target) in enumerate(parts)]
    for copy in take:
        copy.start()
    for first, second in zip(take, give):
        first.wait()
        second.start()
    for copy in give:
        copy.wait()


def solution(mesh):
    n = mesh.shape["blk"]
    chunk = 2 * CX // n

    def part(theta, cond, vel, heat, wall, kinds, blocks, rows):
        hbm = pl.BlockSpec(memory_space=pltpu.HBM)
        anywhere = pl.BlockSpec(memory_space=pl.ANY)
        vmem = pl.BlockSpec(memory_space=pltpu.VMEM)
        buf = lambda *shape: pltpu.VMEM(shape, F32)
        held = pl.pallas_call(
            functools.partial(kernel, n),
            out_shape=(
                jax.ShapeDtypeStruct(theta.shape, F32),
                jax.ShapeDtypeStruct(wall.shape, F32),
            ),
            in_specs=[hbm] * 8,
            out_specs=(anywhere, vmem),
            scratch_shapes=[
                buf(4, CY + 2, PAD, LZ),
                buf(CY, PAD, LZ),
                buf(3, CY, ROWS, LZ),
                buf(CY, ROWS, LZ),
                buf(7, CY, ROWS, LZ),
                buf(4, 2, PAD, LZ),
                buf(2, PAD, LZ),
                buf(4, 2, ROWS, LZ),
                buf(7, 2, ROWS, LZ),
                buf(2, ROWS, LZ),
                buf(2, CY, ROWS, LZ),
                buf(2, 2, CY, 8, LZ),
                buf(2, 2, CY, 8, LZ),
                buf(6, CX, LZ),
                buf(6, 8, LZ),
                buf(3, CX, LZ),
                buf(3, CX, LZ),
                buf(2, 3, 8, LZ),
                buf(2, 4, CX, LZ),
                buf(2, 2, 4, 8, LZ),
                buf(CX, LZ),
                buf(CX, LZ),
                buf(2, 8, LZ),
                buf(2, CX, LZ),
                buf(2, CX, LZ),
                buf(2, 2, 8, LZ),
                buf(2, 8, LZ),
                buf(2, 8, LZ),
                buf(2, 2, 8, LZ),
                buf(2, 2, 8, LZ),
                buf(2, CY, 8, LZ),
                buf(n, chunk, LZ),
                buf(2, n, chunk, LZ),
                pltpu.VMEM((2 * CX, CX), jnp.bfloat16),
                pltpu.VMEM((CX, 2 * CX), jnp.bfloat16),
                pltpu.SMEM((n,), jnp.int32),
                pltpu.VMEM((1, CX), jnp.int32),
                pltpu.VMEM((1, CX), jnp.int32),
                pltpu.SemaphoreType.DMA((8,)),
                pltpu.SemaphoreType.DMA((5,)),
                pltpu.SemaphoreType.DMA((5,)),
                pltpu.SemaphoreType.DMA((5,)),
                pltpu.SemaphoreType.DMA((5,)),
                pltpu.SemaphoreType.DMA((2, 5)),
                pltpu.SemaphoreType.DMA((2, 5)),
                pltpu.SemaphoreType.DMA((2, 5)),
                pltpu.SemaphoreType.DMA((2, 5)),
                pltpu.SemaphoreType.DMA((2,)),
                pltpu.SemaphoreType.DMA((2,)),
                pltpu.SemaphoreType.REGULAR((2,)),
            ],
            compiler_params=pltpu.CompilerParams(
                collective_id=0, has_side_effects=True, vmem_limit_bytes=56 * 2**20
            ),
        )(theta, cond, vel, heat, wall, kinds, blocks, rows)
        return pl.pallas_call(
            publish,
            out_shape=tuple(jax.ShapeDtypeStruct(x.shape, F32) for x in held),
            in_specs=[anywhere] * 2,
            out_specs=(anywhere, anywhere),
            scratch_shapes=[
                buf(CY, CX, LZ),
                buf(CX, LZ),
                pltpu.SemaphoreType.DMA((3,)),
                pltpu.SemaphoreType.DMA((3,)),
            ],
        )(*held)

    whole = P("blk", None, None, "span")
    rows = P("blk", None, "span")
    return jax.shard_map(
        part,
        mesh=mesh,
        in_specs=(whole, whole, P("blk", None, None, None, "span"), whole, rows, P(), P("blk", None), P("blk", None)),
        out_specs=(whole, rows),
        check_vma=False,
    )
```

```python
import functools

import jax
import jax.numpy as jnp
from jax import lax
from jax.experimental import pallas as pl
from jax.experimental.pallas import tpu as pltpu
from jax.sharding import PartitionSpec as P

MESH = pl.DeviceIdType.MESH
ITERS, SWEEPS = 2, 3
CY, CX, LZ = 16, 128, 128
LOW = 4
TILES = CX // 8 + 1
ROWS = 8 * TILES
PAD = ROWS + 16
F32 = jnp.float32
AW, AE, AS, AN, AB, AA, AD, SRC = range(8)


def tile(i, shift=0):
    return pl.ds(8 + 8 * i + shift, 8)


def row8(i):
    return pl.ds(8 * i, 8)


def remote(src, dst, send, recv, device):
    return pltpu.make_async_remote_copy(
        src_ref=src, dst_ref=dst, send_sem=send, recv_sem=recv, device_id=device, device_id_type=MESH
    )


def split3(x):
    hi = x.astype(jnp.bfloat16)
    rest = x - hi.astype(F32)
    mid = rest.astype(jnp.bfloat16)
    low = (rest - mid.astype(F32)).astype(jnp.bfloat16)
    return hi, mid, low


def pick(chooser, x):
    return sum(jnp.dot(chooser, part, preferred_element_type=F32) for part in split3(x))


def kernel(
    n, theta_ref, cond_ref, vel_ref, heat_ref, wall_ref, kind_ref, block_ref, row_ref,
    theta_out, wall_out,
    th, kb, vb, hb, co, st, sk, sv, sco, sw, pz,
    xs, xr, qo, hq, qs, qr, cr, qx, cx, qa, qar, ca, qt, qtr, ct, qw, qwr, wx, wc, tr,
    sb, rb, choose_send, choose_recv, kinds, blocks, rows,
    load_sem, low_send, low_recv, rest_send, rest_recv, wall_send, wall_recv, theta_send, theta_recv,
    many_send, many_recv, known,
):
    b, s = lax.axis_index("blk"), lax.axis_index("span")
    chunk = 2 * CX // n
    east, west = lax.rem(b + 1, n), lax.rem(b + n - 1, n)
    E, W, Z, ZE, ZW = (east, s), (west, s), (b, 1 - s), (east, 1 - s), (west, 1 - s)
    own, planes = pl.ds(8, CX), pl.ds(1, CY)

    def line(count, stride):
        at = lax.rem(b // stride, count)
        return [(b + (lax.rem(at + d, count) - at) * stride, s) for d in range(1, count)]

    line_z, line_x, line_y = line(n // 16, 16), line(4, 4), line(4, 1)
    barrier = pltpu.get_barrier_semaphore()
    beside = [E, W, Z, ZE, ZW] + line_z + line_x + line_y
    for peer in beside:
        pl.semaphore_signal(barrier, inc=1, device_id=peer, device_id_type=MESH)

    loads = [
        pltpu.make_async_copy(kind_ref, kinds, load_sem.at[5]),
        pltpu.make_async_copy(block_ref, blocks, load_sem.at[6]),
        pltpu.make_async_copy(row_ref, rows, load_sem.at[7]),
        pltpu.make_async_copy(theta_ref.at[0], th.at[0, planes, own], load_sem.at[0]),
        pltpu.make_async_copy(cond_ref.at[0], kb.at[:, own], load_sem.at[1]),
        pltpu.make_async_copy(vel_ref.at[0], vb.at[:, :, pl.ds(0, CX)], load_sem.at[2]),
        pltpu.make_async_copy(heat_ref.at[0], hb.at[:, pl.ds(0, CX)], load_sem.at[3]),
        pltpu.make_async_copy(wall_ref.at[0], th.at[0, 0, own], load_sem.at[4]),
    ]
    for load in loads:
        load.start()

    rb[:, pl.ds(b, 1)] = jnp.zeros((2, 1, chunk, LZ), F32)

    lane = lax.broadcasted_iota(jnp.int32, (8, LZ), 1)
    sub = lax.broadcasted_iota(jnp.int32, (8, LZ), 0)
    group, place = lane // 8, lane % 8
    first_lane, last_lane = lane == 0, lane == LZ - 1
    low_half = place < 4
    middle = (place >= 2) & (place < 6)
    near = sub < 4
    last = TILES - 1

    for t in range(4):
        th[t, CY + 1] = jnp.zeros((PAD, LZ), F32)

    for load in loads:
        load.wait()
    fluid = kinds[b].astype(F32)
    metal = 1.0 - fluid
    same_west = 1.0 - jnp.abs(kinds[west].astype(F32) - fluid)
    same_east = 1.0 - jnp.abs(kinds[east].astype(F32) - fluid)

    def edges(load, count=CY):
        out = pltpu.roll(load(0), 4, 1)
        for y in range(1, count):
            out = jnp.where(group == y, pltpu.roll(load(y), (8 * y + 4) % LZ, 1), out)
        return out

    def pack_static(at, at_pad, count=CY):
        q_k = edges(lambda y: kb[y, at_pad], count)
        q_v = [edges(lambda y, d=d: vb[d, y, at], count) for d in range(3)]
        q_h = edges(lambda y: hb[y, at], count)
        return [q_k] + q_v + [q_h]

    def beside_middle(x):
        return jnp.where(place >= 6, pltpu.roll(x, 4, 1), pltpu.roll(x, LZ - 4, 1))

    def from_beside(x):
        return jnp.where(low_half, pltpu.roll(x, LZ - 4, 1), pltpu.roll(x, 4, 1))

    def paired(q):
        return [
            q[0],
            jnp.where(middle, q[1], beside_middle(q[2])),
            jnp.where(middle, q[3], beside_middle(q[4])),
        ]

    def pack_low(i, carry):
        at = pl.ds(pl.multiple_of(8 * i, 8), 8)
        at_pad = pl.ds(pl.multiple_of(8 * i + 8, 8), 8)
        q = pack_static(at, at_pad, LOW) + [edges(lambda y: th[0, y + 1, at_pad], LOW)]
        sent = [q[5]] + paired(q)
        out = sent[0]
        for slot in range(1, 4):
            out = jnp.where(group >= LOW * slot, pltpu.roll(sent[slot], 8 * LOW * slot, 1), out)
        qa[at] = out
        return carry

    def pack_tile(i, carry):
        at = pl.ds(pl.multiple_of(8 * i, 8), 8)
        at_pad = pl.ds(pl.multiple_of(8 * i + 8, 8), 8)
        q = pack_static(at, at_pad) + [edges(lambda y: th[0, y + 1, at_pad])]
        sent = [q[5]] + paired(q)
        rest = [jnp.where(group < LOW, pltpu.roll(sent[3], LZ - 32 * (m + 1), 1), sent[m]) for m in range(3)]
        for slot in range(6):
            qo[slot, at] = q[slot]
        for slot in range(3):
            qs[slot, at] = rest[slot]
        return carry

    lax.fori_loop(0, TILES - 1, pack_low, 0, unroll=4)

    def pack_rows(y, carry):
        end, pad_end = pl.ds(CX - 8, 8), pl.ds(CX, 8)
        xs[0, 0, y] = jnp.where(sub >= 5, th[0, y + 1, pad_end], pltpu.roll(kb[y, pad_end], 5, 0))
        xs[0, 1, y] = jnp.where(
            sub >= 6,
            vb[0, y, end],
            jnp.where(
                sub >= 4,
                pltpu.roll(vb[1, y, end], 6, 0),
                jnp.where(sub >= 2, pltpu.roll(vb[2, y, end], 4, 0), pltpu.roll(hb[y, end], 2, 0)),
            ),
        )
        zero, pad_zero = pl.ds(0, 8), pl.ds(8, 8)
        xs[1, 0, y] = jnp.where(sub < 3, th[0, y + 1, pad_zero], pltpu.roll(kb[y, pad_zero], 3, 0))
        xs[1, 1, y] = jnp.where(
            sub < 2,
            vb[0, y, zero],
            jnp.where(
                sub < 4,
                pltpu.roll(vb[1, y, zero], 2, 0),
                jnp.where(sub < 6, pltpu.roll(vb[2, y, zero], 4, 0), pltpu.roll(hb[y, zero], 6, 0)),
            ),
        )
        return carry

    lax.fori_loop(0, CY, pack_rows, 0, unroll=4)

    def pack_wall(r, t):
        out = pltpu.roll(th[t, 0, tile(0)], 4, 1)
        for i in range(1, TILES - 1):
            out = jnp.where(group == i, pltpu.roll(th[t, 0, tile(i)], (8 * i + 4) % LZ, 1), out)
        qw[r] = out

    pack_wall(0, 0)

    pl.semaphore_wait(barrier, len(beside))
    for peer in line_x:
        pl.semaphore_signal(known.at[0], inc=1, device_id=peer, device_id_type=MESH)

    def wall_copies(r, t):
        plane, ss, rs = th.at[t, 0], wall_send.at[r], wall_recv.at[r]
        tail, head = plane.at[pl.ds(CX, 8)], plane.at[pl.ds(8, 8)]
        return [
            remote(tail, wc.at[r, 0], ss.at[3], rs.at[3], ZE),
            remote(head, wc.at[r, 1], ss.at[4], rs.at[4], ZW),
            remote(tail, wx.at[r, 0], ss.at[0], rs.at[0], E),
            remote(head, wx.at[r, 1], ss.at[1], rs.at[1], W),
            remote(qw.at[r], qwr.at[r], ss.at[2], rs.at[2], Z),
        ]

    head, tail = pl.ds(0, 8), pl.ds(CX - 8, 8)
    low, rest = pl.ds(0, LOW), pl.ds(LOW, CY - LOW)

    def theta_copies(late):
        ss, rs = theta_send.at[late], theta_recv.at[late]
        at, to = (pl.ds(1 + LOW, CY - LOW), pl.ds(LOW, CY - LOW)) if late else (pl.ds(1, LOW), low)
        return [
            remote(qt.at[late, tail], ct.at[late, 0], ss.at[1], rs.at[1], ZE),
            remote(qt.at[late, head], ct.at[late, 1], ss.at[2], rs.at[2], ZW),
            remote(th.at[3, at, pl.ds(CX, 8)], tr.at[0, to], ss.at[3], rs.at[3], E),
            remote(th.at[3, at, pl.ds(8, 8)], tr.at[1, to], ss.at[4], rs.at[4], W),
            remote(qt.at[late], qtr.at[late], ss.at[0], rs.at[0], Z),
        ]

    low_copies = [
        remote(qa.at[tail], ca.at[0], low_send.at[3], low_recv.at[3], ZE),
        remote(qa.at[head], ca.at[1], low_send.at[4], low_recv.at[4], ZW),
        remote(xs.at[0, :, low], xr.at[0, :, low], low_send.at[0], low_recv.at[0], E),
        remote(xs.at[1, :, low], xr.at[1, :, low], low_send.at[1], low_recv.at[1], W),
        remote(qa, qar, low_send.at[2], low_recv.at[2], Z),
    ]
    rest_copies = [
        remote(qs.at[:, tail], cr.at[0], rest_send.at[3], rest_recv.at[3], ZE),
        remote(qs.at[:, head], cr.at[1], rest_send.at[4], rest_recv.at[4], ZW),
        remote(xs.at[0, :, rest], xr.at[0, :, rest], rest_send.at[0], rest_recv.at[0], E),
        remote(xs.at[1, :, rest], xr.at[1, :, rest], rest_send.at[1], rest_recv.at[1], W),
        remote(qs, qr, rest_send.at[2], rest_recv.at[2], Z),
    ]
    for copy in low_copies + wall_copies(0, 0):
        copy.start()

    lax.fori_loop(0, TILES - 1, pack_tile, 0, unroll=2)
    for copy in rest_copies:
        copy.start()

    mine = jnp.broadcast_to(blocks[...].astype(F32), (CX, CX))
    theirs = jnp.broadcast_to(rows[...].astype(F32), (CX, CX))
    mine_t, theirs_t = mine.T, theirs.T
    at_row = lax.broadcasted_iota(jnp.int32, (CX, CX), 0)
    at_col = lax.broadcasted_iota(jnp.int32, (CX, CX), 1)
    alike = mine_t == mine
    rank = jnp.sum(jnp.where(alike & (at_row < at_col), 1.0, 0.0), axis=0, keepdims=True)
    code = (chunk * mine[0:1] + rank).astype(jnp.int32)
    choose_send[...] = jnp.where(
        lax.broadcasted_iota(jnp.int32, (2 * CX, CX), 0) == code, 1.0, 0.0
    ).astype(jnp.bfloat16)
    rank_t = jnp.sum(jnp.where(alike & (theirs < theirs_t), 1.0, 0.0), axis=1, keepdims=True)
    code_t = (chunk * mine_t[:, 0:1] + rank_t).astype(jnp.int32)
    choose_recv[...] = jnp.where(
        lax.broadcasted_iota(jnp.int32, (CX, 2 * CX), 1) == code_t, 1.0, 0.0
    ).astype(jnp.bfloat16)

    rows_last = row8(last)

    def unpack_rows(y, carry):
        e0, e1, w0, w1 = xr[1, 0, y], xr[1, 1, y], xr[0, 0, y], xr[0, 1, y]
        t = jnp.where(near, e0, w0)
        th[0, y + 1, tile(last)] = t
        th[0, y + 1, tile(-1)] = t
        th[0, y + 1, tile(TILES)] = th[0, y + 1, tile(0)]
        k = jnp.where(near, pltpu.roll(e0, 5, 0), pltpu.roll(w0, 3, 0))
        kb[y, tile(last)] = k
        kb[y, tile(-1)] = k
        kb[y, tile(TILES)] = kb[y, tile(0)]
        vb[0, y, rows_last] = jnp.where(near, e1, w1)
        vb[1, y, rows_last] = jnp.where(near, pltpu.roll(e1, 6, 0), pltpu.roll(w1, 2, 0))
        vb[2, y, rows_last] = jnp.where(near, pltpu.roll(e1, 4, 0), pltpu.roll(w1, 4, 0))
        hb[y, rows_last] = jnp.where(near, pltpu.roll(e1, 2, 0), pltpu.roll(w1, 6, 0))
        return carry

    def put_strip(ref, at, own_q, other_q):
        ref[0, at] = jnp.where(low_half, other_q, own_q)
        ref[1, at] = jnp.where(low_half, own_q, other_q)

    def put_static(at, at_pad, own_q, other_q):
        put_strip(sk, at_pad, own_q[0], other_q[0])
        for slot in range(2):
            t = other_q[1 + slot]
            put_strip(sv.at[2 * slot], at, own_q[1 + 2 * slot], t)
            put_strip(sv.at[2 * slot + 1], at, own_q[2 + 2 * slot], from_beside(t))

    def split(value):
        return [pltpu.roll(value, LZ - 32 * slot, 1) if slot else value for slot in range(4)]

    def join(value, before):
        out = [jnp.where(group < LOW, x, y) for x, y in zip(before, value)]
        fourth = before[3]
        for m in range(3):
            fourth = jnp.where(group >= LOW * (m + 1), pltpu.roll(value[m], 32 * (m + 1), 1), fourth)
        return out + [fourth]

    def take_tiles(late):
        def one(i, carry):
            at = pl.ds(pl.multiple_of(8 * i, 8), 8)
            if late:
                out = join([qr[m, at] for m in range(3)], [qx[0, slot, at] for slot in range(4)])
            else:
                out = split(qar[at])
            for slot, value in enumerate(out):
                qx[late, slot, at] = value
            return carry

        lax.fori_loop(0, TILES - 1, one, 0, unroll=4)

    def take_sides(late):
        for side in range(2):
            if late:
                out = join([cr[side, m] for m in range(3)], [cx[0, side, slot] for slot in range(4)])
            else:
                out = split(ca[side])
            for slot, value in enumerate(out):
                cx[late, side, slot] = value

    def pack_halo(count):
        q = pack_static(rows_last, tile(last), count) + [edges(lambda y: th[0, y + 1, tile(last)], count)]
        for slot in range(6):
            hq[slot] = q[slot]

    def static_tiles(late):
        def one(i, carry):
            at = pl.ds(pl.multiple_of(8 * i, 8), 8)
            at_pad = pl.ds(pl.multiple_of(8 * i + 8, 8), 8)
            put_strip(st.at[0], at_pad, qo[5, at], qx[late, 0, at])
            put_static(at, at_pad, [qo[slot, at] for slot in range(5)], [qx[late, slot, at] for slot in range(1, 4)])
            return carry

        lax.fori_loop(0, TILES - 1, one, 0, unroll=4)

    def static_halo(late):
        other = [jnp.where(near, cx[late, 1, slot], cx[late, 0, slot]) for slot in range(4)]
        put_strip(st.at[0], tile(last), hq[5], other[0])
        put_static(rows_last, tile(last), [hq[slot] for slot in range(5)], other[1:])
        wrap(st.at[0])
        wrap(sk)

    def wrap(ref):
        for side in range(2):
            ref[side, tile(-1)] = ref[side, tile(last)]
            ref[side, tile(TILES)] = ref[side, tile(0)]

    def coefficients(k, k_w, k_e, k_s, k_n, k_b, k_a, v, mask_w, mask_e, bottom, top):
        v = [fluid * x for x in v]
        a_w = mask_w(0.5 * (k + k_w) + jnp.maximum(v[0], 0.0))
        a_e = mask_e(0.5 * (k + k_e) - jnp.minimum(v[0], 0.0))
        a_b = 0.5 * (k + k_b) + jnp.maximum(v[1], 0.0)
        a_b = a_b * (1.0 - metal * bottom)
        a_a = (0.5 * (k + k_a) - jnp.minimum(v[1], 0.0)) * (1.0 - top)
        a_s = 0.5 * (k + k_s) + jnp.maximum(v[2], 0.0)
        a_n = 0.5 * (k + k_n) - jnp.minimum(v[2], 0.0)
        a_d = 1.0 - (a_w + a_e + a_s + a_n + a_b + a_a)
        return a_w, a_e, a_s, a_n, a_b + metal * bottom, a_a, a_d

    whole, whole_w, whole_e = pl.ds(8, ROWS), pl.ds(7, ROWS), pl.ds(9, ROWS)
    strip_row = lax.broadcasted_iota(jnp.int32, (ROWS, LZ), 0)
    strip_group = lax.broadcasted_iota(jnp.int32, (ROWS, LZ), 1) // 8
    strip_first = strip_group == 0

    def strip_coefficients():
        both = []
        for side in range(2):
            k = sk[side, whole]
            both.append(coefficients(
                k, sk[side, whole_w], sk[side, whole_e], pltpu.roll(k, 1, 1), pltpu.roll(k, LZ - 1, 1),
                jnp.where(strip_first, k, pltpu.roll(k, 8, 1)), pltpu.roll(k, LZ - 8, 1),
                [sv[d, side] for d in range(3)],
                lambda x: jnp.where(strip_row == 0, same_west * x, x),
                lambda x: jnp.where(strip_row == CX - 1, same_east * x, x),
                strip_first.astype(F32), (strip_group == CY - 1).astype(F32),
            ))
        for side, a in enumerate(both):
            for slot, value in enumerate(a):
                sco[slot, side] = value

    def plane_coefficients(tiles):
        def one(y, carry):
            bottom = (y == 0).astype(F32)
            top = (y == CY - 1).astype(F32)
            below, above = jnp.maximum(y - 1, 0), jnp.minimum(y + 1, CY - 1)
            for i in tiles:
                k = kb[y, tile(i)]
                k_s, k_n = pltpu.roll(k, 1, 1), pltpu.roll(k, LZ - 1, 1)
                mask_w = (lambda x: jnp.where(sub == 0, same_west * x, x)) if i == 0 else (lambda x: x)
                mask_e = (lambda x: jnp.where(sub == 7, same_east * x, x)) if i == last - 1 else (lambda x: x)
                a = coefficients(
                    k, kb[y, tile(i, -1)], kb[y, tile(i, 1)], k_s, k_n, kb[below, tile(i)], kb[above, tile(i)],
                    [vb[d, y, row8(i)] for d in range(3)], mask_w, mask_e, bottom, top,
                )
                for slot, value in enumerate(a):
                    co[slot, y, row8(i)] = value
            return carry

        return one

    inner = plane_coefficients(range(1, last - 1))
    outer = plane_coefficients((0, last - 1, last))

    lax.fori_loop(0, CY, inner, 0, unroll=2)

    low_copies[4].wait()
    take_tiles(0)
    static_tiles(0)
    for copy in low_copies[:4]:
        copy.wait()
    pl.semaphore_wait(known.at[0], len(line_x))
    for peer in line_y:
        pl.semaphore_signal(known.at[1], inc=1, device_id=peer, device_id_type=MESH)

    edge_two, edge_one = (lane < 2) | (lane >= LZ - 2), first_lane | last_lane

    def sweep(t, following, step, first, end, size):
        def some(g, carry):
            for m in range(size):
                y = size * g + m
                for i in range(TILES):
                    at = row8(i)
                    c = th[t, y + 1, tile(i)]
                    new = (
                        (hb[y, at] + co[AD, y, at] * c)
                        + (co[AW, y, at] * th[t, y + 1, tile(i, -1)] + co[AE, y, at] * th[t, y + 1, tile(i, 1)])
                        + (co[AS, y, at] * pltpu.roll(c, 1, 1) + co[AN, y, at] * pltpu.roll(c, LZ - 1, 1))
                        + (co[AB, y, at] * th[t, y, tile(i)] + co[AA, y, at] * th[t, y + 2, tile(i)])
                    )
                    if step > 0:
                        new = jnp.where(edge_two if step == 1 else edge_one, pz[step - 1, y, at], new)
                    th[following, y + 1, tile(i)] = new
                    if i == last:
                        th[following, y + 1, tile(-1)] = new
                    if i == 0:
                        th[following, y + 1, tile(TILES)] = new
            return carry

        lax.fori_loop(first, end, some, 0)

    first_group = group == 0

    def strip_sweeps():
        for step in range(SWEEPS):
            for side in range(2):
                for i in range(TILES):
                    at = row8(i)
                    c = st[step, side, tile(i)]
                    below = jnp.where(first_group, sw[side, at], pltpu.roll(c, 8, 1))
                    new = (
                        (sv[3, side, at] + sco[AD, side, at] * c)
                        + (sco[AW, side, at] * st[step, side, tile(i, -1)] + sco[AE, side, at] * st[step, side, tile(i, 1)])
                        + (sco[AS, side, at] * pltpu.roll(c, 1, 1) + sco[AN, side, at] * pltpu.roll(c, LZ - 1, 1))
                        + (sco[AB, side, at] * below + sco[AA, side, at] * pltpu.roll(c, LZ - 8, 1))
                    )
                    st[step + 1, side, tile(i)] = new
                    if i == last:
                        st[step + 1, side, tile(-1)] = new
                    if i == 0:
                        st[step + 1, side, tile(TILES)] = new

    def spread(slot, first, end):
        strips = [jnp.where(low_half, st[slot + 2, 1, tile(i)], st[slot + 2, 0, tile(i)]) for i in range(TILES)]
        for y in range(first, end):
            for i in range(TILES):
                pz[slot, y, row8(i)] = pltpu.roll(strips[i], 124 - 8 * y, 1)

    def send_faces(r, t):
        field, wall = th[t, 1, own], th[t, 0, own]
        sent = fluid * (kb[0, own] * (field - wall)) + metal * field
        sb[...] = pick(choose_send[...], sent).reshape(n, chunk, LZ)

        def to(zd, i):
            x, y, c = (b // 4) % 4 + 3 - i // 4, (b // 2) % 2 + 1 - (i // 2) % 2, b % 2 + 1 - i % 2
            z = lax.rem(b // 16 + zd, n // 16)
            t = z * 16 + lax.rem(x, 4) * 4 + lax.rem(y, 2) * 2 + lax.rem(c, 2)
            remote(sb.at[t], rb.at[r, b], many_send.at[r], many_recv.at[r], (t, s)).start()

        for zd in (4, 3, 5, 2, 6, 1, 7):
            if zd < n // 16:
                lax.fori_loop(0, 16, lambda i, carry, zd=zd: (to(zd, i), carry)[1], 0, unroll=2)
        lax.fori_loop(0, 15, lambda i, carry: (to(0, i), carry)[1], 0, unroll=3)

    def receive_faces(r):
        others = pl.ds(0, n - 1)
        remote(sb.at[others], rb.at[r, others], many_send.at[r], many_recv.at[r], Z).wait()
        return pick(choose_recv[...], rb[r].reshape(2 * CX, LZ))

    def wall_strip(r):
        wall_last = jnp.where(near, wx[r, 1], wx[r, 0])
        th[3 * r, 0, tile(last)] = wall_last
        wall = th[3 * r, 0, whole]
        for t in range(4):
            if t != 3 * r:
                th[t, 0, whole] = wall
        q = qwr[r]
        for i in range(TILES - 1):
            other = pltpu.roll(q, LZ - 8 * i, 1) if i else q
            put_strip(sw, row8(i), pltpu.roll(wall[8 * i : 8 * i + 8], 4, 1), other)
        put_strip(
            sw, rows_last, pltpu.roll(wall_last, 4, 1), pltpu.roll(jnp.where(near, wc[r, 1], wc[r, 0]), 4, 1)
        )

    def theta_strips(late):
        def one(i, carry):
            at = pl.ds(pl.multiple_of(8 * i, 8), 8)
            put_strip(st.at[0], pl.ds(pl.multiple_of(8 * i + 8, 8), 8), qt[late, at], qtr[late, at])
            return carry

        lax.fori_loop(0, TILES - 1, one, 0, unroll=4)
        put_strip(
            st.at[0], tile(last), edges(lambda y: th[3, y + 1, tile(last)], CY if late else LOW), jnp.where(near, ct[late, 1], ct[late, 0])
        )
        wrap(st.at[0])

    def unpack_theta(y, carry):
        t = jnp.where(near, tr[1, y], tr[0, y])
        th[3, y + 1, tile(last)] = t
        th[3, y + 1, tile(-1)] = t
        return carry

    def send_theta(late):
        def pack(i, carry):
            at_pad = pl.ds(pl.multiple_of(8 * i + 8, 8), 8)
            at = pl.ds(pl.multiple_of(8 * i, 8), 8)
            qt[late, at] = edges(lambda y: th[3, y + 1, at_pad], CY if late else LOW)
            return carry

        lax.fori_loop(0, TILES - 1, pack, 0, unroll=4)
        for copy in theta_copies(late):
            copy.start()

    store = pltpu.make_async_copy(th.at[2, planes, own], theta_out.at[0], load_sem.at[0])

    def early_sweeps(r):
        for step, pairs in enumerate((2, 1, 1)):
            sweep((3 * r + step) % 4, (3 * r + step + 1) % 4, step, 0, pairs, 2)

    def late_sweeps(r):
        for step in range(SWEEPS):
            sweep((3 * r + step) % 4, (3 * r + step + 1) % 4, step, 0, CY // 4, 4)

    def when(p, value, action):
        pl.when(p == value)(action)

    def unpack(take, first, end):
        lax.fori_loop(first, end, take, 0, unroll=4)

    def spread_both(first, end):
        for slot in range(2):
            spread(slot, first, end)

    for copy in wall_copies(0, 0):
        copy.wait()
    wall_strip(0)

    def first_iteration(p, carry):
        @pl.when(p == 0)
        def _():
            take_sides(0)
            unpack(unpack_rows, 0, LOW)
            pack_halo(LOW)
            lax.fori_loop(0, LOW, outer, 0, unroll=4)

        @pl.when(p == 1)
        def _():
            for copy in rest_copies:
                copy.wait()
            take_tiles(1)
            take_sides(1)
            static_tiles(1)
            unpack(unpack_rows, LOW, CY)
            pack_halo(CY)
            lax.fori_loop(0, CY, outer, 0, unroll=4)

        static_halo(p)
        strip_coefficients()
        strip_sweeps()
        when(p, 0, lambda: spread_both(0, 4))
        when(p, 1, lambda: spread_both(0, CY))
        when(p, 0, lambda: early_sweeps(0))
        when(p, 1, lambda: late_sweeps(0))

        @pl.when(p == 0)
        def _():
            pl.semaphore_wait(known.at[1], len(line_y))
            send_faces(0, 3)

        return carry

    lax.fori_loop(0, 2, first_iteration, 0)

    send_theta(0)
    th[3, 0, own] = receive_faces(0)
    pack_wall(1, 3)
    for copy in wall_copies(1, 3):
        copy.start()
    send_theta(1)
    for copy in theta_copies(0):
        copy.wait()
    unpack(unpack_theta, 0, LOW)
    theta_strips(0)
    for copy in wall_copies(1, 3):
        copy.wait()
    wall_strip(1)

    def second_iteration(p, carry):
        @pl.when(p == 1)
        def _():
            for copy in theta_copies(1):
                copy.wait()
            unpack(unpack_theta, LOW, CY)
            theta_strips(1)

        strip_sweeps()
        when(p, 0, lambda: spread_both(0, 4))
        when(p, 1, lambda: spread_both(0, CY))
        when(p, 0, lambda: early_sweeps(1))
        when(p, 1, lambda: late_sweeps(1))

        @pl.when(p == 0)
        def _():
            send_faces(1, 2)

        return carry

    lax.fori_loop(0, 2, second_iteration, 0)
    store.start()
    th[2, 0, own] = receive_faces(1)
    wall_out[0] = th[2, 0, own]
    store.wait()


def publish(theta, wall, theta_out, wall_out, field, rows, come, go):
    half = pl.ds(0, CY // 2), pl.ds(CY // 2, CY // 2)
    parts = [(theta.at[0, at], field.at[at], theta_out.at[0, at]) for at in half]
    parts.append((wall.at[0], rows, wall_out.at[0]))
    take = [pltpu.make_async_copy(source, here, come.at[i]) for i, (source, here, _) in enumerate(parts)]
    give = [pltpu.make_async_copy(here, target, go.at[i]) for i, (_, here, target) in enumerate(parts)]
    for copy in take:
        copy.start()
    for first, second in zip(take, give):
        first.wait()
        second.start()
    for copy in give:
        copy.wait()


def solution(mesh):
    n = mesh.shape["blk"]
    chunk = 2 * CX // n

    def part(theta, cond, vel, heat, wall, kinds, blocks, rows):
        hbm = pl.BlockSpec(memory_space=pltpu.HBM)
        anywhere = pl.BlockSpec(memory_space=pl.ANY)
        vmem = pl.BlockSpec(memory_space=pltpu.VMEM)
        buf = lambda *shape: pltpu.VMEM(shape, F32)
        held = pl.pallas_call(
            functools.partial(kernel, n),
            out_shape=(
                jax.ShapeDtypeStruct(theta.shape, F32),
                jax.ShapeDtypeStruct(wall.shape, F32),
            ),
            in_specs=[hbm] * 8,
            out_specs=(anywhere, vmem),
            scratch_shapes=[
                buf(4, CY + 2, PAD, LZ),
                buf(CY, PAD, LZ),
                buf(3, CY, ROWS, LZ),
                buf(CY, ROWS, LZ),
                buf(7, CY, ROWS, LZ),
                buf(4, 2, PAD, LZ),
                buf(2, PAD, LZ),
                buf(4, 2, ROWS, LZ),
                buf(7, 2, ROWS, LZ),
                buf(2, ROWS, LZ),
                buf(2, CY, ROWS, LZ),
                buf(2, 2, CY, 8, LZ),
                buf(2, 2, CY, 8, LZ),
                buf(6, CX, LZ),
                buf(6, 8, LZ),
                buf(3, CX, LZ),
                buf(3, CX, LZ),
                buf(2, 3, 8, LZ),
                buf(2, 4, CX, LZ),
                buf(2, 2, 4, 8, LZ),
                buf(CX, LZ),
                buf(CX, LZ),
                buf(2, 8, LZ),
                buf(2, CX, LZ),
                buf(2, CX, LZ),
                buf(2, 2, 8, LZ),
                buf(2, 8, LZ),
                buf(2, 8, LZ),
                buf(2, 2, 8, LZ),
                buf(2, 2, 8, LZ),
                buf(2, CY, 8, LZ),
                buf(n, chunk, LZ),
                buf(2, n, chunk, LZ),
                pltpu.VMEM((2 * CX, CX), jnp.bfloat16),
                pltpu.VMEM((CX, 2 * CX), jnp.bfloat16),
                pltpu.SMEM((n,), jnp.int32),
                pltpu.VMEM((1, CX), jnp.int32),
                pltpu.VMEM((1, CX), jnp.int32),
                pltpu.SemaphoreType.DMA((8,)),
                pltpu.SemaphoreType.DMA((5,)),
                pltpu.SemaphoreType.DMA((5,)),
                pltpu.SemaphoreType.DMA((5,)),
                pltpu.SemaphoreType.DMA((5,)),
                pltpu.SemaphoreType.DMA((2, 5)),
                pltpu.SemaphoreType.DMA((2, 5)),
                pltpu.SemaphoreType.DMA((2, 5)),
                pltpu.SemaphoreType.DMA((2, 5)),
                pltpu.SemaphoreType.DMA((2,)),
                pltpu.SemaphoreType.DMA((2,)),
                pltpu.SemaphoreType.REGULAR((2,)),
            ],
            compiler_params=pltpu.CompilerParams(
                collective_id=0, has_side_effects=True, vmem_limit_bytes=56 * 2**20
            ),
        )(theta, cond, vel, heat, wall, kinds, blocks, rows)
        return pl.pallas_call(
            publish,
            out_shape=tuple(jax.ShapeDtypeStruct(x.shape, F32) for x in held),
            in_specs=[anywhere] * 2,
            out_specs=(anywhere, anywhere),
            scratch_shapes=[
                buf(CY, CX, LZ),
                buf(CX, LZ),
                pltpu.SemaphoreType.DMA((3,)),
                pltpu.SemaphoreType.DMA((3,)),
            ],
        )(*held)

    whole = P("blk", None, None, "span")
    rows = P("blk", None, "span")
    return jax.shard_map(
        part,
        mesh=mesh,
        in_specs=(whole, whole, P("blk", None, None, None, "span"), whole, rows, P(), P("blk", None), P("blk", None)),
        out_specs=(whole, rows),
        check_vma=False,
    )
```
